512 devices in a mesh: slab: 32 (over z, core), work: 16 (over y, x).
Axes of the slice: x: 4, y: 4, z: 16, core: 2. Of those that a mesh axis runs over, the one named last changes fastest.
Arguments:
- volume: bfloat16 [1024, 24576], P(('slab', 'work')), may hold values from -6 to 6
- tissue: int32 [1024], P(('slab', 'work')), may hold values from 0 to 1, as said below
- w_first: bfloat16 [24, 1, 3, 3, 3], replicated, may hold values from -1.25 to 1.25
- w_second: bfloat16 [24, 24, 3, 3, 3], replicated, may hold values from -0.25 to 0.25
- w_down: bfloat16 [48, 24, 3, 3, 3], replicated, may hold values from -0.25 to 0.25
- w_up: bfloat16 [24, 48], replicated, may hold values from -0.875 to 0.875
- w_out: bfloat16 [3, 24], replicated, may hold values from -1.25 to 1.25
Outputs:
- boundary: bfloat16 [1024, 3, 16384], P(('slab', 'work'))
The draws below stay inside these ranges and needn't reach their ends.
Inputs may be any that keep to these rules, and one draw needn't show every extreme that they name: Of the 32 bricks of each slab exactly half hold tissue.
All inputs are finite; a program needn't handle non-finite values.
Results may differ from the reference program's by a relative error of at most 0.0045.
Values may be sent and summed in bfloat16 or wider, within the bound.
No kernel may reach another device: no remote copies, remote signals or barrier semaphores. Data moves between devices by JAX's collectives and lax.ppermute only.
A program may use at most 128 MiB of HBM per device.

```python
import jax
import jax.numpy as jnp
from jax import lax

SIDE = 32
DEPTH = 16
MARGIN = 4
EXTENT = 24
CHANNELS = 24
COARSE = 48
CLASSES = 3
GROUP = 32
SLABS = 32
BRICKS = 1024


def draw_tissue(key, part):
    key = jax.random.fold_in(key, 3)
    slab_keys = jax.random.split(key, SLABS)
    orders = jax.vmap(lambda k: jax.random.permutation(k, GROUP))(slab_keys)
    return (orders < GROUP // 2).astype(jnp.int32).reshape(BRICKS)


def levels(stream_key, shape, cuts, smallest, top_value):
    loudness = 1.0
    for axis_at, shards_of in cuts:
        steps = jax.random.uniform(jax.random.fold_in(jax.random.fold_in(stream_key, 6), axis_at), (shards_of,), jnp.float32, smallest / len(cuts), top_value / len(cuts))
        loudness = loudness * jnp.repeat(jnp.exp(steps), shape[axis_at] // shards_of).reshape((-1,) + (1,) * (len(shape) - 1 - axis_at))
    return loudness


def bell_draw(key, extent, spread, most, cuts=(), held_as=jnp.bfloat16):
    drawn = spread * jax.random.normal(key, extent, jnp.float32)
    if cuts:
        drawn = drawn * levels(key, extent, cuts, -0.22, 0.18)
    return jnp.clip(drawn, -most, most).astype(held_as)


def setup_inputs(seed: int = 0) -> dict:
    keys = jax.random.split(jax.random.key(seed), 8)
    volume = bell_draw(keys[0], (BRICKS, EXTENT * SIDE * SIDE), 1.0, 6.0, ((0, 512),))
    tissue = draw_tissue(jax.random.fold_in(keys[7], 71), 0)
    w_first = bell_draw(keys[2], (CHANNELS, 1, 3, 3, 3), 27 ** -0.5, 1.25)
    w_second = bell_draw(keys[3], (CHANNELS, CHANNELS, 3, 3, 3), (27 * CHANNELS) ** -0.5, 0.25)
    w_down = bell_draw(keys[4], (COARSE, CHANNELS, 3, 3, 3), (27 * CHANNELS) ** -0.5, 0.25)
    w_up = bell_draw(keys[5], (CHANNELS, COARSE), COARSE ** -0.5, 0.875)
    w_out = bell_draw(keys[6], (CLASSES, CHANNELS), CHANNELS ** -0.5, 1.25)
    return dict(volume=volume, tissue=tissue, w_first=w_first, w_second=w_second, w_down=w_down, w_up=w_up, w_out=w_out)


def conv3(x, w):
    return lax.conv_general_dilated(x, w, (1, 1, 1), "SAME", dimension_numbers=("NCDHW", "OIDHW", "NCDHW"), preferred_element_type=jnp.float32)


def network(bricks, w_first, w_second, w_down, w_up, w_out):
    count = bricks.shape[0]
    field = bricks.reshape(count, 1, EXTENT, SIDE, SIDE)
    first = jax.nn.relu(conv3(field, w_first)).astype(jnp.bfloat16)
    fine = jax.nn.relu(conv3(first, w_second)).astype(jnp.bfloat16)
    cubes = fine.reshape(count, CHANNELS, EXTENT // 2, 2, SIDE // 2, 2, SIDE // 2, 2)
    pooled = jnp.max(cubes, axis=(3, 5, 7))
    downsampled_features = jax.nn.relu(conv3(pooled, w_down)).astype(jnp.bfloat16)
    lifted = jnp.einsum("oc,ncxyz->noxyz", w_up.astype(jnp.float32), downsampled_features.astype(jnp.float32))
    mixed = cubes.astype(jnp.float32) + lifted[:, :, :, None, :, None, :, None]
    mixed = jax.nn.relu(mixed).astype(jnp.bfloat16).reshape(count, CHANNELS, EXTENT * SIDE * SIDE)
    logits = jnp.einsum("oc,ncv->nov", w_out.astype(jnp.float32), mixed.astype(jnp.float32))
    return jax.nn.sigmoid(logits).astype(jnp.bfloat16).reshape(count, CLASSES, EXTENT, SIDE * SIDE)


def reference(volume, tissue, w_first, w_second, w_down, w_up, w_out):
    live_rows = jnp.nonzero(tissue, size=BRICKS // 2)[0].astype(jnp.int32)

    def evaluate(rows):
        return network(volume[rows], w_first, w_second, w_down, w_up, w_out)

    live_pred = lax.map(evaluate, live_rows.reshape(-1, 8))
    live_pred = live_pred.reshape(BRICKS // 2, CLASSES, EXTENT, SIDE * SIDE)
    preds = jnp.zeros((BRICKS, CLASSES, EXTENT, SIDE * SIDE), jnp.bfloat16).at[live_rows].set(live_pred)
    preds = preds.reshape(SLABS, GROUP, CLASSES, EXTENT, SIDE * SIDE)
    core = preds[:, :, :, MARGIN:MARGIN + DEPTH].astype(jnp.float32)
    upper = preds[:, :, :, MARGIN + DEPTH:].astype(jnp.float32)
    lower = preds[:, :, :, :MARGIN].astype(jnp.float32)
    blank = jnp.zeros((1, GROUP, CLASSES, MARGIN, SIDE * SIDE), jnp.float32)
    from_below = jnp.concatenate([blank, upper[:-1]], axis=0)
    from_above = jnp.concatenate([lower[1:], blank], axis=0)
    total = core + jnp.pad(from_below, ((0, 0), (0, 0), (0, 0), (0, DEPTH - MARGIN), (0, 0)))
    total = total + jnp.pad(from_above, ((0, 0), (0, 0), (0, 0), (DEPTH - MARGIN, 0), (0, 0)))
    return total.astype(jnp.bfloat16).reshape(BRICKS, CLASSES, DEPTH * SIDE * SIDE)
```

```python
import functools

import jax
import jax.numpy as jnp
from jax import lax
from jax.experimental import pallas as pl
from jax.experimental.pallas import tpu as pltpu
from jax.sharding import PartitionSpec as P

SIDE = 32
DEPTH = 16
MARGIN = 4
EXTENT = 24
CHANNELS = 24
COARSE = 48
CLASSES = 3
OWNED = 2
HALF = EXTENT // 2
LANES = 256
PLANE = SIDE * SIDE
VROWS = 48
HROWS = 16 * CHANNELS
PROWS = 224
BIG = -1e30

f32 = jnp.float32
bf16 = jnp.bfloat16


def dot(a, b):
    return jnp.dot(a, b, preferred_element_type=f32)


def iota(shape, dim):
    return lax.broadcasted_iota(jnp.int32, shape, dim)


def shifted(x, sy, sx, yy, xx):
    if sx:
        x = pltpu.roll(x, (-sx) % LANES, 1)
        x = jnp.where(xx == (15 if sx > 0 else 0), 0.0, x)
    if sy:
        x = pltpu.roll(x, (-16 * sy) % LANES, 1)
        x = jnp.where(yy == (15 if sy > 0 else 0), 0.0, x)
    return x


def swap_chunks(parts, low):
    out = []
    for j in range(4):
        halves = []
        for d in range(2):
            piece = [parts[2 * d + i][:, 128 * (j // 2) : 128 * (j // 2) + 128] for i in range(2)]
            if j % 2 == 0:
                halves.append(jnp.where(low, piece[0], pltpu.roll(piece[1], 64, 1)))
            else:
                halves.append(jnp.where(low, pltpu.roll(piece[0], 64, 1), piece[1]))
        out.append(jnp.concatenate(halves, axis=1))
    return out


def unet(
    tissue, vol, w1, w2, wd, wup, wout,
    core, low_out, high_out,
    t1, b2, td, w1big, w2big, wd3, wo, vs, vz, hx, fs, ys, rs,
):
    lane = iota((1, LANES), 1)
    yy, xx = lane >> 4, lane & 15
    low64 = iota((1, 128), 1) < 64

    t1[...] = jnp.zeros_like(t1)
    for kz in range(3):
        for ky in range(3):
            t1[kz * 48 + ky * 8 : kz * 48 + ky * 8 + 3, 0:CHANNELS] = w1[kz * 3 + ky].astype(f32)
    base1 = t1[...].T[0:CHANNELS]
    for pz in range(2):
        for ey in range(4):
            for half in range(2):
                rows = []
                for ex in (2 * half, 2 * half + 1):
                    s = pz * 48 + ey * 8 + ex
                    m = pltpu.roll(base1, s, 1) if s else base1
                    for on, col in ((ey == 0, 6), (ey == 3, 7), (ex == 0, 14), (ex == 3, 15)):
                        if on:
                            m = jnp.where(lane == col, BIG, m)
                    rows.append(m)
                at = (pz * 16 + ey * 4 + 2 * half) * CHANNELS
                w1big[at : at + 48] = jnp.concatenate(rows, axis=0)[:, 0:192].astype(bf16)

    b2[...] = jnp.zeros_like(b2)
    for kz in range(3):
        for ky in range(3):
            at = kz * HROWS + ky * 96
            b2[:, at : at + 72] = jnp.concatenate(
                [w2[kz * 9 + ky * 3 + kx].astype(f32) for kx in range(3)], axis=1
            )
    base2 = b2[...]
    for oz in range(2):
        for oy in range(2):
            rows = []
            for ox in range(2):
                s = oz * HROWS + oy * 96 + ox * 24
                rows.append(pltpu.roll(base2, s, 1) if s else base2)
            at = (oz * 4 + oy * 2) * CHANNELS
            w2big[at : at + 48] = jnp.concatenate(rows, axis=0).astype(bf16)

    td[...] = jnp.zeros_like(td)
    for kz in range(3):
        for k in range(9):
            td[kz, k * 24 : k * 24 + 24, 0:COARSE] = wd[kz * 9 + k].astype(f32)
    for kz in range(3):
        wd3[kz * COARSE : kz * COARSE + COARSE] = td[kz].T[0:COARSE, 0:PROWS].astype(bf16)

    ci = iota((CHANNELS, 192), 0)
    col = iota((CHANNELS, 192), 1)
    tiled = dot(wout[...], (col % 24 == ci).astype(bf16))
    r = iota((32, 192), 0)
    c = iota((32, 192), 1) // 24
    acc = jnp.zeros((32, 192), f32)
    for cls in range(CLASSES):
        acc = acc + jnp.where((r & 3) == cls, tiled[cls : cls + 1], 0.0)
    wo[...] = jnp.where(c == ((r >> 2) & 1) * 4 + (r >> 3), acc, 0.0).astype(bf16)

    def source(l):
        p = l >> 6
        return ((l >> 4) & 3) * 64 + (p >> 1) * 32 + (l & 15) * 2 + (p & 1)

    sort = (iota((LANES, LANES), 0) == source(lane)).astype(bf16)
    unsort = (iota((LANES, LANES), 1) == source(iota((LANES, 1), 0))).astype(bf16)

    for z in range(EXTENT):
        for t in range(4):
            at = z * PLANE + t * LANES
            for d in range(2):
                vs[d, pl.ds(t * EXTENT + z, OWNED, stride=96), :] = vol[
                    :, at + 128 * d : at + 128 * d + 128
                ].astype(f32)
    sorted_cells = dot(jnp.concatenate([vs[0], vs[1]], axis=1).astype(bf16), sort)
    zero_plane = jnp.zeros((VROWS, LANES), f32)
    for b in range(OWNED):
        vz[b] = jnp.zeros((2, 26 * VROWS, 128), f32)
        parts = [sorted_cells[b * 96 + t * 24 : b * 96 + t * 24 + 24] for t in range(4)]
        parities = swap_chunks(parts, low64)
        for p in range(4):
            for sy in (-1, 0, 1):
                for sx in (-1, 0, 1):
                    row = (2 * sy + (p >> 1) + 2) * 8 + 2 * sx + (p & 1) + 2
                    near = shifted(parities[p], sy, sx, yy, xx)
                    for d in range(2):
                        vz[b, d, pl.ds(VROWS + row, EXTENT, stride=VROWS), :] = near[
                            :, 128 * d : 128 * d + 128
                        ]
        for row, m in ((6, yy == 0), (7, yy == 15), (14, xx == 0), (15, xx == 15)):
            for d in range(2):
                vz[b, d, pl.ds(row, 26, stride=VROWS), :] = jnp.broadcast_to(
                    m[:, 128 * d : 128 * d + 128].astype(f32), (26, 128)
                )
        hx[b, 0:HROWS] = jnp.zeros((HROWS, LANES), bf16)
        hx[b, 25 * HROWS : 26 * HROWS] = jnp.zeros((HROWS, LANES), bf16)
        ys[b, 0] = jnp.zeros((144, LANES), f32)
        ys[b, HALF + 1] = jnp.zeros((144, LANES), f32)

    def first(i, carry):
        for b in range(OWNED):
            at = pl.multiple_of(i * (2 * VROWS), 2 * VROWS)
            near = [vz[b, d, pl.ds(at, 4 * VROWS), :] for d in range(2)]
            near = jnp.concatenate(near, axis=1).astype(bf16)
            out = jnp.maximum(dot(w1big[...], near), 0.0).astype(bf16)
            to = pl.multiple_of(i * (2 * HROWS), HROWS) + HROWS
            hx[b, pl.ds(pl.multiple_of(to, HROWS), 2 * HROWS), :] = out
        return carry

    lax.fori_loop(0, HALF, first, 0)

    def second(i, carry):
        for b in range(OWNED):
            at = pl.multiple_of(i * (2 * HROWS), 2 * HROWS)
            fine = jnp.maximum(dot(w2big[...], hx[b, pl.ds(at, 4 * HROWS), :]), 0.0)
            fs[b, i] = fine.astype(bf16)
            p = functools.reduce(jnp.maximum, [fine[c * 24 : c * 24 + 24] for c in range(8)])
            near = [shifted(p, sy, sx, yy, xx) for sy in (-1, 0, 1) for sx in (-1, 0, 1)]
            near = jnp.concatenate(near + [jnp.zeros((8, LANES), f32)], axis=0).astype(bf16)
            ys[b, i + 1] = dot(wd3[...], near)
        return carry

    lax.fori_loop(0, HALF, second, 0)

    def third(i, carry):
        for b in range(OWNED):
            g = ys[b, i, 0:48] + ys[b, i + 1, 48:96] + ys[b, i + 2, 96:144]
            u = dot(wup[...], jnp.maximum(g, 0.0).astype(bf16))
            fine = fs[b, i].astype(f32).reshape(8, CHANNELS, LANES)
            z = jnp.maximum(fine + u[None], 0.0).reshape(8 * CHANNELS, LANES).astype(bf16)
            pred = jax.nn.sigmoid(dot(wo[...], z))
            pred = jnp.where(tissue[b] == 1, pred, 0.0)
            at = pl.multiple_of(i * 8, 8)
            for p in range(4):
                rs[b, p, pl.ds(at, 8), :] = pred[p * 8 : p * 8 + 8]
        return carry

    lax.fori_loop(0, HALF, third, 0)

    for b in range(OWNED):
        chunks = swap_chunks([rs[b, p] for p in range(4)], low64)
        for t in range(4):
            rows = dot(chunks[t].astype(bf16), unsort).astype(bf16)
            rows = rows.astype(f32)
            for z in range(EXTENT):
                at = (z // 2) * 8 + (z % 2) * 4
                piece = rows[at : at + CLASSES].astype(bf16)
                if z < MARGIN:
                    to, ref = z, low_out
                elif z < MARGIN + DEPTH:
                    to, ref = z - MARGIN, core
                else:
                    to, ref = z - MARGIN - DEPTH, high_out
                ref[b, :, to * PLANE + t * LANES : to * PLANE + t * LANES + LANES] = piece


def border_sum(core, below, above, out):
    edge = MARGIN * PLANE
    full = DEPTH * PLANE
    out[:, :, edge : full - edge] = core[:, :, edge : full - edge]
    out[:, :, 0:edge] = (core[:, :, 0:edge].astype(f32) + below[...].astype(f32)).astype(bf16)
    out[:, :, full - edge :] = (
        core[:, :, full - edge :].astype(f32) + above[...].astype(f32)
    ).astype(bf16)


VMEM = pl.BlockSpec(memory_space=pltpu.VMEM)
SMEM = pl.BlockSpec(memory_space=pltpu.SMEM)


def evaluate(volume, tissue, w_first, w_second, w_down, w_up, w_out):
    w1 = jnp.transpose(w_first, (1, 2, 3, 4, 0)).reshape(9, 3, CHANNELS)
    w2 = jnp.transpose(w_second, (2, 3, 4, 0, 1)).reshape(27, CHANNELS, CHANNELS)
    wd = jnp.transpose(w_down, (2, 3, 4, 1, 0)).reshape(27, CHANNELS, COARSE)
    edge = jax.ShapeDtypeStruct((OWNED, CLASSES, MARGIN * PLANE), bf16)
    return pl.pallas_call(
        unet,
        out_shape=(jax.ShapeDtypeStruct((OWNED, CLASSES, DEPTH * PLANE), bf16), edge, edge),
        in_specs=[SMEM] + [VMEM] * 6,
        out_specs=(VMEM,) * 3,
        scratch_shapes=[
            pltpu.VMEM((256, 128), f32),
            pltpu.VMEM((CHANNELS, 4 * HROWS), f32),
            pltpu.VMEM((3, 256, 128), f32),
            pltpu.VMEM((2 * HROWS, 192), bf16),
            pltpu.VMEM((192, 4 * HROWS), bf16),
            pltpu.VMEM((144, PROWS), bf16),
            pltpu.VMEM((32, 192), bf16),
            pltpu.VMEM((2, 192, 128), f32),
            pltpu.VMEM((OWNED, 2, 26 * VROWS, 128), f32),
            pltpu.VMEM((OWNED, 26 * HROWS, LANES), bf16),
            pltpu.VMEM((OWNED, HALF, 192, LANES), bf16),
            pltpu.VMEM((OWNED, HALF + 2, 144, LANES), f32),
            pltpu.VMEM((OWNED, 4, HALF * 8, LANES), f32),
        ],
        compiler_params=pltpu.CompilerParams(vmem_limit_bytes=48 << 20),
    )(tissue, volume, w1, w2, wd, w_up, w_out)


def shards(volume, tissue, w_first, w_second, w_down, w_up, w_out):
    core, low, high = evaluate(volume, tissue, w_first, w_second, w_down, w_up, w_out)
    slabs = lax.axis_size("slab")
    up = [(i, i + 1) for i in range(slabs - 1)]
    down = [(i + 1, i) for i in range(slabs - 1)]
    below = lax.ppermute(high, "slab", up)
    above = lax.ppermute(low, "slab", down)
    return pl.pallas_call(
        border_sum,
        out_shape=jax.ShapeDtypeStruct(core.shape, bf16),
        in_specs=[VMEM] * 3,
        out_specs=VMEM,
    )(core, below, above)


def solution(mesh):
    return jax.shard_map(
        shards,
        mesh=mesh,
        in_specs=(P(("slab", "work"), None), P(("slab", "work")), P(), P(), P(), P(), P()),
        out_specs=P(("slab", "work"), None, None),
        check_vma=False,
    )
```

```python
import functools

import jax
import jax.numpy as jnp
from jax import lax
from jax.experimental import pallas as pl
from jax.experimental.pallas import tpu as pltpu
from jax.sharding import PartitionSpec as P

SIDE = 32
DEPTH = 16
MARGIN = 4
EXTENT = 24
CHANNELS = 24
COARSE = 48
CLASSES = 3
OWNED = 2
HALF = EXTENT // 2
LANES = 256
PLANE = SIDE * SIDE
VROWS = 32
HROWS = 8 * CHANNELS
PROWS = 224
BIG = -1e30
UNROLL = 1

f32 = jnp.float32
bf16 = jnp.bfloat16


def dot(a, b):
    return jnp.dot(a, b, preferred_element_type=f32)


def iota(shape, dim):
    return lax.broadcasted_iota(jnp.int32, shape, dim)


def along_x(x, sx, xx):
    x = [pltpu.roll(x[:, 128 * d : 128 * d + 128], (-sx) % 128, 1) for d in range(2)]
    return jnp.where(xx == (15 if sx > 0 else 0), 0.0, jnp.concatenate(x, axis=1))


def along_y(x, sy, yy):
    x = [pltpu.roll(x[:, 128 * d : 128 * d + 128], (-16 * sy) % 128, 1) for d in range(2)]
    zero = jnp.zeros_like(x[0])
    edge = yy[:, 0:128] == (7 if sy > 0 else 0)
    low = jnp.where(edge, x[1] if sy > 0 else zero, x[0])
    high = jnp.where(edge, zero if sy > 0 else x[0], x[1])
    return jnp.concatenate([low, high], axis=1)


def shifted(x, sy, sx, yy, xx):
    x = along_x(x, sx, xx) if sx else x
    return along_y(x, sy, yy) if sy else x


def swap_chunks(parts, low):
    out = []
    for j in range(4):
        halves = []
        for d in range(2):
            piece = [parts[2 * d + i][:, 128 * (j // 2) : 128 * (j // 2) + 128] for i in range(2)]
            if j % 2 == 0:
                halves.append(jnp.where(low, piece[0], pltpu.roll(piece[1], 64, 1)))
            else:
                halves.append(jnp.where(low, pltpu.roll(piece[0], 64, 1), piece[1]))
        out.append(jnp.concatenate(halves, axis=1))
    return out


def unet(*refs):
    hbm, (core, low_out, high_out), local = refs[:7], refs[7:10], refs[10:17]
    sems = refs[17]
    copies = [pltpu.make_async_copy(a, c, sems.at[k]) for k, (a, c) in enumerate(zip(hbm, local))]
    for copy in copies:
        copy.start()
    evaluate_bricks(copies, *local, core, low_out, high_out, *refs[18:])


def evaluate_bricks(
    copies, tissue, vol, w1, w2, wd, wup, wout, core, low_out, high_out,
    t1, b2, td, w1big, w2big, wd3, wo, vs, vz, hx, fs, ps, px, ys, gs, us, zs, rs,
):
    lane = iota((1, LANES), 1)
    yy, xx = lane >> 4, lane & 15
    low64 = iota((1, 128), 1) < 64

    for b in range(OWNED):
        vz[b] = jnp.zeros((2, 26 * VROWS, 128), f32)
        hx[b, 0:HROWS] = jnp.zeros((HROWS, LANES), bf16)
        hx[b, 25 * HROWS : 26 * HROWS] = jnp.zeros((HROWS, LANES), bf16)
        ys[b, 0] = jnp.zeros((144, LANES), f32)
        ys[b, HALF + 1] = jnp.zeros((144, LANES), f32)
        for row, m in ((24, yy == 0), (25, yy == 15)):
            for d in range(2):
                vz[b, d, pl.ds(row, 26, stride=VROWS), :] = jnp.broadcast_to(
                    m[:, 128 * d : 128 * d + 128].astype(f32), (26, 128)
                )
    t1[...] = jnp.zeros_like(t1)
    b2[...] = jnp.zeros_like(b2)
    td[...] = jnp.zeros_like(td)
    for copy in copies:
        copy.wait()

    for kz in range(3):
        for ky in range(3):
            at = kz * VROWS + ky * 4
            t1[at : at + 3, 0:CHANNELS] = w1[kz * 3 + ky].astype(f32)
    base1 = t1[...].T[0:CHANNELS]
    for pz in range(2):
        for ey in range(4):
            rows = []
            for ox in range(2):
                s = pz * VROWS + ey * 4 + ox
                m = pltpu.roll(base1, s, 1) if s else base1
                if ey in (0, 3):
                    m = jnp.where(lane[:, 0:128] == (24 if ey == 0 else 25), BIG, m)
                rows.append(m)
            at = (pz * 8 + ey * 2) * CHANNELS
            w1big[at : at + 48] = jnp.concatenate(rows, axis=0).astype(bf16)

    for ox in range(4):
        for kz in range(3):
            for ky in range(3):
                piece = [
                    w2[kz * 9 + ky * 3 + 2 - ox + dx].astype(f32)
                    if 0 <= 2 - ox + dx < 3
                    else jnp.zeros((CHANNELS, CHANNELS), f32)
                    for dx in range(2)
                ]
                at = kz * HROWS + ky * 48
                b2[ox, :, at : at + 48] = jnp.concatenate(piece, axis=1)
    for ox in range(4):
        base2 = b2[ox]
        for oz in range(2):
            rows = []
            for oy in range(2):
                s = oz * HROWS + oy * 48
                rows.append(pltpu.roll(base2, s, 1) if s else base2)
            at = (ox * 4 + oz * 2) * CHANNELS
            w2big[at : at + 48] = jnp.concatenate(rows, axis=0).astype(bf16)

    for kz in range(3):
        for k in range(9):
            td[kz, k * 24 : k * 24 + 24, 0:COARSE] = wd[kz * 9 + k].astype(f32)
    for kz in range(3):
        wd3[kz * COARSE : kz * COARSE + COARSE] = td[kz].T[0:COARSE, 0:PROWS].astype(bf16)

    ci = iota((CHANNELS, 192), 0)
    col = iota((CHANNELS, 192), 1)
    tiled = dot(wout[...], (col % 24 == ci).astype(bf16))
    r = iota((32, 192), 0)
    c = iota((32, 192), 1) // 24
    acc = jnp.zeros((32, 192), f32)
    for cls in range(CLASSES):
        acc = acc + jnp.where((r & 3) == cls, tiled[cls : cls + 1], 0.0)
    cell = ((r >> 3) & 1) * 4 + ((r >> 2) & 1) * 2 + (r >> 4)
    wo[...] = jnp.where(c == cell, acc, 0.0).astype(bf16)

    def source(l):
        p = l >> 6
        return ((l >> 4) & 3) * 64 + (p >> 1) * 32 + (l & 15) * 2 + (p & 1)

    sort = (iota((LANES, LANES), 0) == source(lane)).astype(bf16)
    unsort = (iota((LANES, LANES), 1) == source(iota((LANES, 1), 0))).astype(bf16)

    for z in range(EXTENT):
        for t in range(4):
            at = z * PLANE + t * LANES
            for d in range(2):
                vs[d, pl.ds(t * EXTENT + z, OWNED, stride=96), :] = vol[
                    :, at + 128 * d : at + 128 * d + 128
                ].astype(f32)
    sorted_cells = dot(jnp.concatenate([vs[0], vs[1]], axis=1).astype(bf16), sort)
    for b in range(OWNED):
        parts = [sorted_cells[b * 96 + t * 24 : b * 96 + t * 24 + 24] for t in range(4)]
        parities = swap_chunks(parts, low64)
        for p in range(4):
            for sy in (-1, 0, 1):
                for sx in ((0, 1) if p & 1 == 0 else (-1, 0)):
                    row = (2 * sy + (p >> 1) + 2) * 4 + 2 * sx + (p & 1) + 1
                    near = shifted(parities[p], sy, sx, yy, xx)
                    for d in range(2):
                        vz[b, d, pl.ds(VROWS + row, EXTENT, stride=VROWS), :] = near[
                            :, 128 * d : 128 * d + 128
                        ]

    def first(j):
        b, i = j // HALF, j % HALF
        at = i * (2 * VROWS)
        if not isinstance(j, int):
            at = pl.multiple_of(at, 2 * VROWS)
        near = [vz[b, d, pl.ds(at, 4 * VROWS), :] for d in range(2)]
        near = jnp.concatenate(near, axis=1).astype(bf16)
        out = jnp.maximum(dot(w1big[...], near), 0.0).astype(bf16)
        to = i * (2 * HROWS) + HROWS
        if not isinstance(j, int):
            to = pl.multiple_of(to, HROWS)
        hx[b, pl.ds(to, 2 * HROWS), :] = out

    def second(j):
        b, i = j // HALF, j % HALF
        at = i * (2 * HROWS)
        if not isinstance(j, int):
            at = pl.multiple_of(at, 2 * HROWS)
        out = dot(w2big[...], hx[b, pl.ds(at, 4 * HROWS), :])
        left = out[96:192] + along_x(out[288:384], -1, xx)
        right = out[192:288] + along_x(out[0:96], 1, xx)
        fine = jnp.maximum(jnp.concatenate([left, right], axis=0), 0.0)
        fs[b, i] = fine.astype(bf16)
        ps[j] = functools.reduce(jnp.maximum, [fine[c * 24 : c * 24 + 24] for c in range(8)])

    def spread(j):
        p = ps[j]
        near = [shifted(p, sy, sx, yy, xx) for sy in (-1, 0, 1) for sx in (-1, 0, 1)]
        near = jnp.concatenate(near + [jnp.zeros((8, LANES), f32)], axis=0).astype(bf16)
        px[j] = near

    def coarse(j):
        b, i = j // HALF, j % HALF
        ys[b, i + 1] = dot(wd3[...], px[j])

    def gather(j):
        b, i = j // HALF, j % HALF
        g = ys[b, i, 0:48] + ys[b, i + 1, 48:96] + ys[b, i + 2, 96:144]
        gs[j] = jnp.maximum(g, 0.0).astype(bf16)

    def lift(j):
        us[j] = dot(wup[...], gs[j])

    def mix(j):
        b, i = j // HALF, j % HALF
        fine = fs[b, i].astype(f32).reshape(8, CHANNELS, LANES)
        z = jnp.maximum(fine + us[j][None], 0.0).reshape(8 * CHANNELS, LANES)
        zs[j] = z.astype(bf16)

    def project(j):
        b, i = j // HALF, j % HALF
        pred = jax.nn.sigmoid(dot(wo[...], zs[j]))
        pred = jnp.where(tissue[b] == 1, pred, 0.0)
        for p in range(4):
            for d in range(2):
                rs[p, d, pl.ds(i * 16 + b, 8, stride=2), :] = pred[
                    p * 8 : p * 8 + 8, 128 * d : 128 * d + 128
                ]

    units = OWNED * HALF

    stages = ((second, 0), (first, 2), (coarse, -2), (lift, -5), (project, -7), (spread, -1), (gather, -4), (mix, -6))
    for j in range(-2, units + 7):
        for stage, lag in stages:
            if 0 <= j + lag < units:
                stage(j + lag)

    chunks = swap_chunks([jnp.concatenate([rs[p, 0], rs[p, 1]], axis=1) for p in range(4)], low64)
    for t in range(4):
        rows = dot(chunks[t].astype(bf16), unsort)
        for z in range(EXTENT):
            if z < MARGIN:
                to, ref = z, low_out
            elif z < MARGIN + DEPTH:
                to, ref = z - MARGIN, core
            else:
                to, ref = z - MARGIN - DEPTH, high_out
            for cls in range(CLASSES):
                piece = rows[z * 8 + cls * 2 : z * 8 + cls * 2 + 2].astype(bf16)
                ref[cls, :, to * PLANE + t * LANES : to * PLANE + t * LANES + LANES] = piece


VMEM = pl.BlockSpec(memory_space=pltpu.VMEM)


def evaluate(volume, tissue, w_first, w_second, w_down, w_up, w_out):
    w1 = jnp.transpose(w_first, (1, 2, 3, 4, 0)).reshape(9, 3, CHANNELS)
    w2 = jnp.transpose(w_second, (2, 3, 4, 0, 1)).reshape(27, CHANNELS, CHANNELS)
    wd = jnp.transpose(w_down, (2, 3, 4, 1, 0)).reshape(27, CHANNELS, COARSE)
    edge = jax.ShapeDtypeStruct((CLASSES, OWNED, MARGIN * PLANE), bf16)
    arrays = [pltpu.with_memory_space_constraint(a, pltpu.HBM) for a in (tissue, volume, w1, w2, wd, w_up, w_out)]
    return pl.pallas_call(
        unet,
        out_shape=(jax.ShapeDtypeStruct((CLASSES, OWNED, DEPTH * PLANE), bf16), edge, edge),
        in_specs=[pl.BlockSpec(memory_space=pltpu.HBM)] * 7,
        out_specs=(VMEM,) * 3,
        scratch_shapes=[pltpu.SMEM(tissue.shape, tissue.dtype)]
        + [pltpu.VMEM(a.shape, a.dtype) for a in arrays[1:]]
        + [
            pltpu.SemaphoreType.DMA((7,)),
            pltpu.VMEM((128, 128), f32),
            pltpu.VMEM((4, CHANNELS, 4 * HROWS), f32),
            pltpu.VMEM((3, 256, 128), f32),
            pltpu.VMEM((2 * HROWS, 4 * VROWS), bf16),
            pltpu.VMEM((384, 4 * HROWS), bf16),
            pltpu.VMEM((144, PROWS), bf16),
            pltpu.VMEM((32, 192), bf16),
            pltpu.VMEM((2, 192, 128), f32),
            pltpu.VMEM((OWNED, 2, 26 * VROWS, 128), f32),
            pltpu.VMEM((OWNED, 26 * HROWS, LANES), bf16),
            pltpu.VMEM((OWNED, HALF, 192, LANES), bf16),
            pltpu.VMEM((OWNED * HALF, CHANNELS, LANES), f32),
            pltpu.VMEM((OWNED * HALF, PROWS, LANES), bf16),
            pltpu.VMEM((OWNED, HALF + 2, 144, LANES), f32),
            pltpu.VMEM((OWNED * HALF, COARSE, LANES), bf16),
            pltpu.VMEM((OWNED * HALF, CHANNELS, LANES), f32),
            pltpu.VMEM((OWNED * HALF, 8 * CHANNELS, LANES), bf16),
            pltpu.VMEM((4, 2, EXTENT * 8, 128), f32),
        ],
        compiler_params=pltpu.CompilerParams(vmem_limit_bytes=48 << 20),
    )(*arrays)


def shards(volume, tissue, w_first, w_second, w_down, w_up, w_out):
    core, low, high = evaluate(volume, tissue, w_first, w_second, w_down, w_up, w_out)
    slabs = lax.axis_size("slab")
    up = [(i, i + 1) for i in range(slabs - 1)]
    down = [(i + 1, i) for i in range(slabs - 1)]
    below = lax.ppermute(high, "slab", up)
    above = lax.ppermute(low, "slab", down)
    rest = DEPTH * PLANE - MARGIN * PLANE
    total = core.astype(f32)
    total = total + jnp.pad(below.astype(f32), ((0, 0), (0, 0), (0, rest)))
    total = total + jnp.pad(above.astype(f32), ((0, 0), (0, 0), (rest, 0)))
    return jnp.transpose(total.astype(bf16), (1, 0, 2))


def solution(mesh):
    return jax.shard_map(
        shards,
        mesh=mesh,
        in_specs=(P(("slab", "work"), None), P(("slab", "work")), P(), P(), P(), P(), P()),
        out_specs=P(("slab", "work"), None, None),
        check_vma=False,
    )
```

```python
import functools

import jax
import jax.numpy as jnp
from jax import lax
from jax.experimental import pallas as pl
from jax.experimental.pallas import tpu as pltpu
from jax.sharding import PartitionSpec as P

SIDE = 32
DEPTH = 16
MARGIN = 4
EXTENT = 24
CHANNELS = 24
COARSE = 48
CLASSES = 3
OWNED = 2
HALF = EXTENT // 2
LANES = 256
PLANE = SIDE * SIDE
VROWS = 32
HROWS = 8 * CHANNELS
PROWS = 224
BIG = -1e30
NAMES = ("volume", "first", "second", "coarse", "up", "out", "tissue")
f32 = jnp.float32
bf16 = jnp.bfloat16


def dot(a, b):
    return jnp.dot(a, b, preferred_element_type=f32)


def iota(shape, dim):
    return lax.broadcasted_iota(jnp.int32, shape, dim)


def along_x(x, sx, xx):
    x = [pltpu.roll(x[:, 128 * d : 128 * d + 128], (-sx) % 128, 1) for d in range(2)]
    return jnp.where(xx == (15 if sx > 0 else 0), 0.0, jnp.concatenate(x, axis=1))


def along_y(x, sy, yy):
    x = [pltpu.roll(x[:, 128 * d : 128 * d + 128], (-16 * sy) % 128, 1) for d in range(2)]
    zero = jnp.zeros_like(x[0])
    edge = yy[:, 0:128] == (7 if sy > 0 else 0)
    low = jnp.where(edge, x[1] if sy > 0 else zero, x[0])
    high = jnp.where(edge, zero if sy > 0 else x[0], x[1])
    return jnp.concatenate([low, high], axis=1)


def shifted(x, sy, sx, yy, xx):
    x = along_x(x, sx, xx) if sx else x
    return along_y(x, sy, yy) if sy else x


def swap_chunks(parts, low):
    out = []
    for j in range(4):
        halves = []
        for d in range(2):
            piece = [parts[2 * d + i][:, 128 * (j // 2) : 128 * (j // 2) + 128] for i in range(2)]
            if j % 2 == 0:
                halves.append(jnp.where(low, piece[0], pltpu.roll(piece[1], 64, 1)))
            else:
                halves.append(jnp.where(low, pltpu.roll(piece[0], 64, 1), piece[1]))
        out.append(jnp.concatenate(halves, axis=1))
    return out


def unet(*refs):
    hbm, (core, low_out, high_out), local = refs[:7], refs[7:10], refs[10:17]
    sems = refs[17]
    copies = [pltpu.make_async_copy(a, c, sems.at[k]) for k, (a, c) in enumerate(zip(hbm, local))]
    for copy in copies:
        copy.start()
    evaluate_bricks(copies, *local, core, low_out, high_out, *refs[18:])


def evaluate_bricks(
    copies, vol, w1, w2, wd, wup, wout, tissue, core, low_out, high_out,
    t1, b2, td, w1big, w2big, wd3, wo, vs, vz, hx, fs, ps, px, ys, gs, us, zs, rs,
):
    lane = iota((1, LANES), 1)
    yy, xx = lane >> 4, lane & 15
    low64 = iota((1, 128), 1) < 64

    for b in range(OWNED):
        vz[b] = jnp.zeros((2, 26 * VROWS, 128), f32)
        hx[b, 0:HROWS] = jnp.zeros((HROWS, LANES), bf16)
        hx[b, 25 * HROWS : 26 * HROWS] = jnp.zeros((HROWS, LANES), bf16)
        ys[b, 0] = jnp.zeros((144, LANES), f32)
        ys[b, HALF + 1] = jnp.zeros((144, LANES), f32)
        for row, m in ((24, yy == 0), (25, yy == 15)):
            for d in range(2):
                vz[b, d, pl.ds(row, 26, stride=VROWS), :] = jnp.broadcast_to(
                    m[:, 128 * d : 128 * d + 128].astype(f32), (26, 128)
                )
    t1[...] = jnp.zeros_like(t1)
    b2[...] = jnp.zeros_like(b2)
    td[...] = jnp.zeros_like(td)
    wait = {name: copy.wait for name, copy in zip(NAMES, copies)}
    wait["volume"]()
    wait["first"]()

    for kz in range(3):
        for ky in range(3):
            at = kz * VROWS + ky * 4
            t1[at : at + 3, 0:CHANNELS] = w1[kz * 3 + ky].astype(f32)
    base1 = t1[...].T[0:CHANNELS]
    for pz in range(2):
        for ey in range(4):
            rows = []
            for ox in range(2):
                s = pz * VROWS + ey * 4 + ox
                m = pltpu.roll(base1, s, 1) if s else base1
                if ey in (0, 3):
                    m = jnp.where(lane[:, 0:128] == (24 if ey == 0 else 25), BIG, m)
                rows.append(m)
            at = (pz * 8 + ey * 2) * CHANNELS
            w1big[at : at + 48] = jnp.concatenate(rows, axis=0).astype(bf16)

    def source(l):
        p = l >> 6
        return ((l >> 4) & 3) * 64 + (p >> 1) * 32 + (l & 15) * 2 + (p & 1)

    sort = (iota((LANES, LANES), 0) == source(lane)).astype(bf16)
    unsort = (iota((LANES, LANES), 1) == source(iota((LANES, 1), 0))).astype(bf16)

    for z in range(EXTENT):
        for t in range(4):
            at = z * PLANE + t * LANES
            for d in range(2):
                vs[d, pl.ds(t * EXTENT + z, OWNED, stride=96), :] = vol[
                    :, at + 128 * d : at + 128 * d + 128
                ].astype(f32)
    sorted_cells = dot(jnp.concatenate([vs[0], vs[1]], axis=1).astype(bf16), sort)
    for b in range(OWNED):
        parts = [sorted_cells[b * 96 + t * 24 : b * 96 + t * 24 + 24] for t in range(4)]
        parities = swap_chunks(parts, low64)
        for p in range(4):
            for sy in (-1, 0, 1):
                for sx in ((0, 1) if p & 1 == 0 else (-1, 0)):
                    row = (2 * sy + (p >> 1) + 2) * 4 + 2 * sx + (p & 1) + 1
                    near = shifted(parities[p], sy, sx, yy, xx)
                    for d in range(2):
                        vz[b, d, pl.ds(VROWS + row, EXTENT, stride=VROWS), :] = near[
                            :, 128 * d : 128 * d + 128
                        ]

    def second_weights():
        wait["second"]()
        for ox in range(4):
            for kz in range(3):
                for ky in range(3):
                    piece = [
                        w2[kz * 9 + ky * 3 + 2 - ox + dx].astype(f32)
                        if 0 <= 2 - ox + dx < 3
                        else jnp.zeros((CHANNELS, CHANNELS), f32)
                        for dx in range(2)
                    ]
                    at = kz * HROWS + ky * 48
                    b2[ox, :, at : at + 48] = jnp.concatenate(piece, axis=1)
        for ox in range(4):
            base2 = b2[ox]
            for oz in range(2):
                rows = []
                for oy in range(2):
                    s = oz * HROWS + oy * 48
                    rows.append(pltpu.roll(base2, s, 1) if s else base2)
                at = (ox * 4 + oz * 2) * CHANNELS
                w2big[at : at + 48] = jnp.concatenate(rows, axis=0).astype(bf16)

    def coarse_weights():
        wait["coarse"]()
        for kz in range(3):
            for k in range(9):
                td[kz, k * 24 : k * 24 + 24, 0:COARSE] = wd[kz * 9 + k].astype(f32)
        for kz in range(3):
            wd3[kz * COARSE : kz * COARSE + COARSE] = td[kz].T[0:COARSE, 0:PROWS].astype(bf16)

    def out_weights():
        wait["up"]()
        wait["out"]()
        wait["tissue"]()
        ci = iota((CHANNELS, 192), 0)
        col = iota((CHANNELS, 192), 1)
        tiled = dot(wout[...], (col % 24 == ci).astype(bf16))
        r = iota((32, 192), 0)
        c = iota((32, 192), 1) // 24
        acc = jnp.zeros((32, 192), f32)
        for cls in range(CLASSES):
            acc = acc + jnp.where((r & 3) == cls, tiled[cls : cls + 1], 0.0)
        cell = ((r >> 3) & 1) * 4 + ((r >> 2) & 1) * 2 + (r >> 4)
        wo[...] = jnp.where(c == cell, acc, 0.0).astype(bf16)

    def first(j):
        b, i = j // HALF, j % HALF
        at = i * (2 * VROWS)
        near = [vz[b, d, pl.ds(at, 4 * VROWS), :] for d in range(2)]
        near = jnp.concatenate(near, axis=1).astype(bf16)
        out = jnp.maximum(dot(w1big[...], near), 0.0).astype(bf16)
        to = i * (2 * HROWS) + HROWS
        hx[b, pl.ds(to, 2 * HROWS), :] = out

    def second(j):
        b, i = j // HALF, j % HALF
        at = i * (2 * HROWS)
        out = dot(w2big[...], hx[b, pl.ds(at, 4 * HROWS), :])
        left = out[96:192] + along_x(out[288:384], -1, xx)
        right = out[192:288] + along_x(out[0:96], 1, xx)
        fine = jnp.maximum(jnp.concatenate([left, right], axis=0), 0.0)
        fs[b, i] = fine.astype(bf16)
        ps[j] = functools.reduce(jnp.maximum, [fine[c * 24 : c * 24 + 24] for c in range(8)])

    def spread(j):
        p = ps[j]
        near = [shifted(p, sy, sx, yy, xx) for sy in (-1, 0, 1) for sx in (-1, 0, 1)]
        near = jnp.concatenate(near + [jnp.zeros((8, LANES), f32)], axis=0).astype(bf16)
        px[j] = near

    def coarse(j):
        b, i = j // HALF, j % HALF
        ys[b, i + 1] = dot(wd3[...], px[j])

    def gather(j):
        b, i = j // HALF, j % HALF
        g = ys[b, i, 0:48] + ys[b, i + 1, 48:96] + ys[b, i + 2, 96:144]
        gs[j] = jnp.maximum(g, 0.0).astype(bf16)

    def lift(j):
        us[j] = dot(wup[...], gs[j])

    def mix(j):
        b, i = j // HALF, j % HALF
        fine = fs[b, i].astype(f32).reshape(8, CHANNELS, LANES)
        z = jnp.maximum(fine + us[j][None], 0.0).reshape(8 * CHANNELS, LANES)
        zs[j] = z.astype(bf16)

    def project(j):
        b, i = j // HALF, j % HALF
        pred = jax.nn.sigmoid(dot(wo[...], zs[j]))
        pred = jnp.where(tissue[b] == 1, pred, 0.0)
        for p in range(4):
            for d in range(2):
                rs[p, d, pl.ds(i * 16 + b, 8, stride=2), :] = pred[
                    p * 8 : p * 8 + 8, 128 * d : 128 * d + 128
                ]

    def emit():
        parts = [jnp.concatenate([rs[p, d] for d in range(2)], axis=1) for p in range(4)]
        chunks = swap_chunks(parts, low64)
        for t in range(4):
            rows = dot(chunks[t].astype(bf16), unsort)
            for z in range(EXTENT):
                if z < MARGIN:
                    to, ref = z, low_out
                elif z < MARGIN + DEPTH:
                    to, ref = z - MARGIN, core
                else:
                    to, ref = z - MARGIN - DEPTH, high_out
                to = to * PLANE + t * LANES
                for cls in range(CLASSES):
                    piece = rows[z * 8 + cls * 2 : z * 8 + cls * 2 + 2]
                    ref[cls, :, to : to + LANES] = piece.astype(bf16)

    units = OWNED * HALF
    second_weights()
    coarse_weights()
    out_weights()
    for j in range(-2, units + 7):
        for stage, lag in (
            (second, 0), (first, 2), (coarse, -2), (lift, -5),
            (project, -7), (spread, -1), (gather, -4), (mix, -6),
        ):
            if 0 <= j + lag < units:
                stage(j + lag)
    emit()


VMEM = pl.BlockSpec(memory_space=pltpu.VMEM)


def evaluate(volume, tissue, w_first, w_second, w_down, w_up, w_out):
    w1 = jnp.transpose(w_first, (1, 2, 3, 4, 0)).reshape(9, 3, CHANNELS)
    w2 = jnp.transpose(w_second, (2, 3, 4, 0, 1)).reshape(27, CHANNELS, CHANNELS)
    wd = jnp.transpose(w_down, (2, 3, 4, 1, 0)).reshape(27, CHANNELS, COARSE)
    edge = jax.ShapeDtypeStruct((CLASSES, OWNED, MARGIN * PLANE), bf16)
    arrays = [pltpu.with_memory_space_constraint(a, pltpu.HBM) for a in (volume, w1, w2, wd, w_up, w_out, tissue)]
    return pl.pallas_call(
        unet,
        out_shape=(jax.ShapeDtypeStruct((CLASSES, OWNED, DEPTH * PLANE), bf16), edge, edge),
        in_specs=[pl.BlockSpec(memory_space=pltpu.HBM)] * 7,
        out_specs=(VMEM,) * 3,
        scratch_shapes=[pltpu.VMEM(a.shape, a.dtype) for a in arrays[:6]]
        + [
            pltpu.SMEM(tissue.shape, tissue.dtype),
            pltpu.SemaphoreType.DMA((7,)),
            pltpu.VMEM((128, 128), f32),
            pltpu.VMEM((4, CHANNELS, 4 * HROWS), f32),
            pltpu.VMEM((3, 256, 128), f32),
            pltpu.VMEM((2 * HROWS, 4 * VROWS), bf16),
            pltpu.VMEM((384, 4 * HROWS), bf16),
            pltpu.VMEM((144, PROWS), bf16),
            pltpu.VMEM((32, 192), bf16),
            pltpu.VMEM((2, 192, 128), f32),
            pltpu.VMEM((OWNED, 2, 26 * VROWS, 128), f32),
            pltpu.VMEM((OWNED, 26 * HROWS, LANES), bf16),
            pltpu.VMEM((OWNED, HALF, 192, LANES), bf16),
            pltpu.VMEM((OWNED * HALF, CHANNELS, LANES), f32),
            pltpu.VMEM((OWNED * HALF, PROWS, LANES), bf16),
            pltpu.VMEM((OWNED, HALF + 2, 144, LANES), f32),
            pltpu.VMEM((OWNED * HALF, COARSE, LANES), bf16),
            pltpu.VMEM((OWNED * HALF, CHANNELS, LANES), f32),
            pltpu.VMEM((OWNED * HALF, 8 * CHANNELS, LANES), bf16),
            pltpu.VMEM((4, 2, EXTENT * 8, 128), f32),
        ],
        compiler_params=pltpu.CompilerParams(vmem_limit_bytes=48 << 20),
    )(*arrays)


def shards(volume, tissue, w_first, w_second, w_down, w_up, w_out):
    core, low, high = evaluate(volume, tissue, w_first, w_second, w_down, w_up, w_out)
    slabs = lax.axis_size("slab")
    me = lax.axis_index("slab")
    odd = (me % 2) == 1
    across = [(i, i + 1) for i in range(1, slabs - 1, 2)] + [(i + 1, i) for i in range(1, slabs - 1, 2)]
    chip = [[i, i + 1] for i in range(0, slabs, 2)]
    two = lax.ppermute(jnp.where(odd, high, low), "slab", across)
    one = lax.all_gather(jnp.where(odd, low, high), "slab", axis_index_groups=chip)
    one = jnp.where(odd, one[0], one[1])
    above = jnp.where(odd, two, one)
    below = jnp.where(odd, one, two)
    rest = DEPTH * PLANE - MARGIN * PLANE
    total = core.astype(f32)
    total = total + jnp.pad(below.astype(f32), ((0, 0), (0, 0), (0, rest)))
    total = total + jnp.pad(above.astype(f32), ((0, 0), (0, 0), (rest, 0)))
    return jnp.transpose(total.astype(bf16), (1, 0, 2))


def solution(mesh):
    return jax.shard_map(
        shards,
        mesh=mesh,
        in_specs=(P(("slab", "work"), None), P(("slab", "work")), P(), P(), P(), P(), P()),
        out_specs=P(("slab", "work"), None, None),
        check_vma=False,
    )
```

```python
import functools

import jax
import jax.numpy as jnp
from jax import lax
from jax.experimental import pallas as pl
from jax.experimental.pallas import tpu as pltpu
from jax.sharding import PartitionSpec as P

SIDE = 32
DEPTH = 16
MARGIN = 4
EXTENT = 24
CHANNELS = 24
COARSE = 48
CLASSES = 3
OWNED = 2
HALF = EXTENT // 2
LANES = 256
PLANE = SIDE * SIDE
VROWS = 32
HROWS = 8 * CHANNELS
PROWS = 224
BIG = -1e30

f32 = jnp.float32
bf16 = jnp.bfloat16


def dot(a, b):
    return jnp.dot(a, b, preferred_element_type=f32)


def iota(shape, dim):
    return lax.broadcasted_iota(jnp.int32, shape, dim)


def along_x(x, sx, xx):
    x = [pltpu.roll(x[:, 128 * d : 128 * d + 128], (-sx) % 128, 1) for d in range(2)]
    return jnp.where(xx == (15 if sx > 0 else 0), 0.0, jnp.concatenate(x, axis=1))


def along_y(x, sy, yy):
    x = [pltpu.roll(x[:, 128 * d : 128 * d + 128], (-16 * sy) % 128, 1) for d in range(2)]
    zero = jnp.zeros_like(x[0])
    edge = yy[:, 0:128] == (7 if sy > 0 else 0)
    low = jnp.where(edge, x[1] if sy > 0 else zero, x[0])
    high = jnp.where(edge, zero if sy > 0 else x[0], x[1])
    return jnp.concatenate([low, high], axis=1)


def shifted(x, sy, sx, yy, xx):
    x = along_x(x, sx, xx) if sx else x
    return along_y(x, sy, yy) if sy else x


def swap_chunks(parts, low):
    out = []
    for j in range(4):
        halves = []
        for d in range(2):
            piece = [parts[2 * d + i][:, 128 * (j // 2) : 128 * (j // 2) + 128] for i in range(2)]
            if j % 2 == 0:
                halves.append(jnp.where(low, piece[0], pltpu.roll(piece[1], 64, 1)))
            else:
                halves.append(jnp.where(low, pltpu.roll(piece[0], 64, 1), piece[1]))
        out.append(jnp.concatenate(halves, axis=1))
    return out


def unet(*refs):
    hbm, (core, low_out, high_out), local = refs[:7], refs[7:10], refs[10:17]
    sems = refs[17]
    copies = [pltpu.make_async_copy(a, c, sems.at[k]) for k, (a, c) in enumerate(zip(hbm, local))]
    for copy in copies:
        copy.start()
    evaluate_bricks(copies, *local, core, low_out, high_out, *refs[18:])


def evaluate_bricks(
    copies, tissue, vol, w1, w2, wd, wup, wout, core, low_out, high_out,
    t1, b2, td, w1big, w2big, wd3, wo, vs, vz, hx, fs, ps, px, ys, gs, us, zs, rs,
):
    lane = iota((1, LANES), 1)
    yy, xx = lane >> 4, lane & 15
    low64 = iota((1, 128), 1) < 64

    rs[...] = jnp.zeros_like(rs)
    for b in range(OWNED):
        vz[b] = jnp.zeros((2, 26 * VROWS, 128), f32)
        hx[b, 0:HROWS] = jnp.zeros((HROWS, LANES), bf16)
        hx[b, 25 * HROWS : 26 * HROWS] = jnp.zeros((HROWS, LANES), bf16)
        ys[b, 0] = jnp.zeros((144, LANES), f32)
        ys[b, HALF + 1] = jnp.zeros((144, LANES), f32)
        for row, m in ((24, yy == 0), (25, yy == 15)):
            for d in range(2):
                vz[b, d, pl.ds(row, 26, stride=VROWS), :] = jnp.broadcast_to(
                    m[:, 128 * d : 128 * d + 128].astype(f32), (26, 128)
                )
    t1[...] = jnp.zeros_like(t1)
    b2[...] = jnp.zeros_like(b2)
    td[...] = jnp.zeros_like(td)
    for copy in copies:
        copy.wait()
    alive = tissue[0] + tissue[1]

    work = functools.partial(
        run, lane, yy, xx, low64, vol, w1, w2, wd, wup, wout, core, low_out, high_out,
        t1, b2, td, w1big, w2big, wd3, wo, vs, vz, hx, fs, ps, px, ys, gs, us, zs, rs,
    )

    @pl.when(alive == 2)
    def _():
        work([0, 1])

    @pl.when(alive == 1)
    def _():
        work([1 - tissue[0]])

    @pl.when(alive == 0)
    def _():
        for ref in (core, low_out, high_out):
            ref[...] = jnp.zeros_like(ref)


def run(
    lane, yy, xx, low64, vol, w1, w2, wd, wup, wout, core, low_out, high_out,
    t1, b2, td, w1big, w2big, wd3, wo, vs, vz, hx, fs, ps, px, ys, gs, us, zs, rs, bricks,
):
    for kz in range(3):
        for ky in range(3):
            at = kz * VROWS + ky * 4
            t1[at : at + 3, 0:CHANNELS] = w1[kz * 3 + ky].astype(f32)
    base1 = t1[...].T[0:CHANNELS]
    for pz in range(2):
        for ey in range(4):
            rows = []
            for ox in range(2):
                s = pz * VROWS + ey * 4 + ox
                m = pltpu.roll(base1, s, 1) if s else base1
                if ey in (0, 3):
                    m = jnp.where(lane[:, 0:128] == (24 if ey == 0 else 25), BIG, m)
                rows.append(m)
            at = (pz * 8 + ey * 2) * CHANNELS
            w1big[at : at + 48] = jnp.concatenate(rows, axis=0).astype(bf16)

    for ox in range(4):
        for kz in range(3):
            for ky in range(3):
                piece = [
                    w2[kz * 9 + ky * 3 + 2 - ox + dx].astype(f32)
                    if 0 <= 2 - ox + dx < 3
                    else jnp.zeros((CHANNELS, CHANNELS), f32)
                    for dx in range(2)
                ]
                at = kz * HROWS + ky * 48
                b2[ox, :, at : at + 48] = jnp.concatenate(piece, axis=1)
    for ox in range(4):
        base2 = b2[ox]
        for oz in range(2):
            rows = []
            for oy in range(2):
                s = oz * HROWS + oy * 48
                rows.append(pltpu.roll(base2, s, 1) if s else base2)
            at = (ox * 4 + oz * 2) * CHANNELS
            w2big[at : at + 48] = jnp.concatenate(rows, axis=0).astype(bf16)

    for kz in range(3):
        for k in range(9):
            td[kz, k * 24 : k * 24 + 24, 0:COARSE] = wd[kz * 9 + k].astype(f32)
    for kz in range(3):
        wd3[kz * COARSE : kz * COARSE + COARSE] = td[kz].T[0:COARSE, 0:PROWS].astype(bf16)

    ci = iota((CHANNELS, 192), 0)
    col = iota((CHANNELS, 192), 1)
    tiled = dot(wout[...], (col % 24 == ci).astype(bf16))
    r = iota((32, 192), 0)
    c = iota((32, 192), 1) // 24
    acc = jnp.zeros((32, 192), f32)
    for cls in range(CLASSES):
        acc = acc + jnp.where((r & 3) == cls, tiled[cls : cls + 1], 0.0)
    cell = ((r >> 3) & 1) * 4 + ((r >> 2) & 1) * 2 + (r >> 4)
    wo[...] = jnp.where(c == cell, acc, 0.0).astype(bf16)

    def source(l):
        p = l >> 6
        return ((l >> 4) & 3) * 64 + (p >> 1) * 32 + (l & 15) * 2 + (p & 1)

    sort = (iota((LANES, LANES), 0) == source(lane)).astype(bf16)
    unsort = (iota((LANES, LANES), 1) == source(iota((LANES, 1), 0))).astype(bf16)

    for z in range(EXTENT):
        for t in range(4):
            at = z * PLANE + t * LANES
            for d in range(2):
                vs[d, pl.ds(t * EXTENT + z, OWNED, stride=96), :] = vol[
                    :, at + 128 * d : at + 128 * d + 128
                ].astype(f32)
    if len(bricks) == OWNED:
        cells = [vs[d] for d in range(2)]
    else:
        cells = [vs[d, pl.ds(pl.multiple_of(bricks[0] * 96, 96), 96), :] for d in range(2)]
    sorted_cells = dot(jnp.concatenate(cells, axis=1).astype(bf16), sort)
    for b in range(len(bricks)):
        parts = [sorted_cells[b * 96 + t * 24 : b * 96 + t * 24 + 24] for t in range(4)]
        parities = swap_chunks(parts, low64)
        for p in range(4):
            for sy in (-1, 0, 1):
                for sx in ((0, 1) if p & 1 == 0 else (-1, 0)):
                    row = (2 * sy + (p >> 1) + 2) * 4 + 2 * sx + (p & 1) + 1
                    near = shifted(parities[p], sy, sx, yy, xx)
                    for d in range(2):
                        vz[b, d, pl.ds(VROWS + row, EXTENT, stride=VROWS), :] = near[
                            :, 128 * d : 128 * d + 128
                        ]

    def first(j):
        b, i = j // HALF, j % HALF
        at = i * (2 * VROWS)
        near = [vz[b, d, pl.ds(at, 4 * VROWS), :] for d in range(2)]
        near = jnp.concatenate(near, axis=1).astype(bf16)
        out = jnp.maximum(dot(w1big[...], near), 0.0).astype(bf16)
        to = i * (2 * HROWS) + HROWS
        hx[b, pl.ds(to, 2 * HROWS), :] = out

    def second(j):
        b, i = j // HALF, j % HALF
        at = i * (2 * HROWS)
        out = dot(w2big[...], hx[b, pl.ds(at, 4 * HROWS), :])
        left = out[96:192] + along_x(out[288:384], -1, xx)
        right = out[192:288] + along_x(out[0:96], 1, xx)
        fine = jnp.maximum(jnp.concatenate([left, right], axis=0), 0.0)
        fs[b, i] = fine.astype(bf16)
        ps[j] = functools.reduce(jnp.maximum, [fine[c * 24 : c * 24 + 24] for c in range(8)])

    def spread(j):
        p = ps[j]
        near = [shifted(p, sy, sx, yy, xx) for sy in (-1, 0, 1) for sx in (-1, 0, 1)]
        near = jnp.concatenate(near + [jnp.zeros((8, LANES), f32)], axis=0).astype(bf16)
        px[j] = near

    def coarse(j):
        b, i = j // HALF, j % HALF
        ys[b, i + 1] = dot(wd3[...], px[j])

    def gather(j):
        b, i = j // HALF, j % HALF
        g = ys[b, i, 0:48] + ys[b, i + 1, 48:96] + ys[b, i + 2, 96:144]
        gs[j] = jnp.maximum(g, 0.0).astype(bf16)

    def lift(j):
        us[j] = dot(wup[...], gs[j])

    def mix(j):
        b, i = j // HALF, j % HALF
        fine = fs[b, i].astype(f32).reshape(8, CHANNELS, LANES)
        z = jnp.maximum(fine + us[j][None], 0.0).reshape(8 * CHANNELS, LANES)
        zs[j] = z.astype(bf16)

    def project(j):
        b, i = j // HALF, j % HALF
        pred = jax.nn.sigmoid(dot(wo[...], zs[j]))
        for p in range(4):
            for d in range(2):
                rs[p, d, pl.ds(i * 16 + bricks[b], 8, stride=2), :] = pred[
                    p * 8 : p * 8 + 8, 128 * d : 128 * d + 128
                ]

    units = len(bricks) * HALF

    stages = ((second, 0), (first, 2), (coarse, -2), (lift, -5), (project, -7), (spread, -1), (gather, -4), (mix, -6))
    for j in range(-2, units + 7):
        for stage, lag in stages:
            if 0 <= j + lag < units:
                stage(j + lag)

    chunks = swap_chunks([jnp.concatenate([rs[p, 0], rs[p, 1]], axis=1) for p in range(4)], low64)
    for t in range(4):
        rows = dot(chunks[t].astype(bf16), unsort)
        for z in range(EXTENT):
            if z < MARGIN:
                to, ref = z, low_out
            elif z < MARGIN + DEPTH:
                to, ref = z - MARGIN, core
            else:
                to, ref = z - MARGIN - DEPTH, high_out
            for cls in range(CLASSES):
                piece = rows[z * 8 + cls * 2 : z * 8 + cls * 2 + 2].astype(bf16)
                ref[cls, :, to * PLANE + t * LANES : to * PLANE + t * LANES + LANES] = piece


VMEM = pl.BlockSpec(memory_space=pltpu.VMEM)


def evaluate(volume, tissue, w_first, w_second, w_down, w_up, w_out):
    w1 = jnp.transpose(w_first, (1, 2, 3, 4, 0)).reshape(9, 3, CHANNELS)
    w2 = jnp.transpose(w_second, (2, 3, 4, 0, 1)).reshape(27, CHANNELS, CHANNELS)
    wd = jnp.transpose(w_down, (2, 3, 4, 1, 0)).reshape(27, CHANNELS, COARSE)
    edge = jax.ShapeDtypeStruct((CLASSES, OWNED, MARGIN * PLANE), bf16)
    arrays = [pltpu.with_memory_space_constraint(a, pltpu.HBM) for a in (tissue, volume, w1, w2, wd, w_up, w_out)]
    return pl.pallas_call(
        unet,
        out_shape=(jax.ShapeDtypeStruct((CLASSES, OWNED, DEPTH * PLANE), bf16), edge, edge),
        in_specs=[pl.BlockSpec(memory_space=pltpu.HBM)] * 7,
        out_specs=(VMEM,) * 3,
        scratch_shapes=[pltpu.SMEM(tissue.shape, tissue.dtype)]
        + [pltpu.VMEM(a.shape, a.dtype) for a in arrays[1:]]
        + [
            pltpu.SemaphoreType.DMA((7,)),
            pltpu.VMEM((128, 128), f32),
            pltpu.VMEM((4, CHANNELS, 4 * HROWS), f32),
            pltpu.VMEM((3, 256, 128), f32),
            pltpu.VMEM((2 * HROWS, 4 * VROWS), bf16),
            pltpu.VMEM((384, 4 * HROWS), bf16),
            pltpu.VMEM((144, PROWS), bf16),
            pltpu.VMEM((32, 192), bf16),
            pltpu.VMEM((2, 192, 128), f32),
            pltpu.VMEM((OWNED, 2, 26 * VROWS, 128), f32),
            pltpu.VMEM((OWNED, 26 * HROWS, LANES), bf16),
            pltpu.VMEM((OWNED, HALF, 192, LANES), bf16),
            pltpu.VMEM((OWNED * HALF, CHANNELS, LANES), f32),
            pltpu.VMEM((OWNED * HALF, PROWS, LANES), bf16),
            pltpu.VMEM((OWNED, HALF + 2, 144, LANES), f32),
            pltpu.VMEM((OWNED * HALF, COARSE, LANES), bf16),
            pltpu.VMEM((OWNED * HALF, CHANNELS, LANES), f32),
            pltpu.VMEM((OWNED * HALF, 8 * CHANNELS, LANES), bf16),
            pltpu.VMEM((4, 2, EXTENT * 8, 128), f32),
        ],
        compiler_params=pltpu.CompilerParams(vmem_limit_bytes=48 << 20),
    )(*arrays)


def shards(volume, tissue, w_first, w_second, w_down, w_up, w_out):
    core, low, high = evaluate(volume, tissue, w_first, w_second, w_down, w_up, w_out)
    slabs = lax.axis_size("slab")
    me = lax.axis_index("slab")
    odd = (me % 2) == 1
    across = [(i, i + 1) for i in range(1, slabs - 1, 2)] + [(i + 1, i) for i in range(1, slabs - 1, 2)]
    chip = [[i, i + 1] for i in range(0, slabs, 2)]
    two = lax.ppermute(jnp.where(odd, high, low), "slab", across)
    one = lax.all_gather(jnp.where(odd, low, high), "slab", axis_index_groups=chip)
    one = jnp.where(odd, one[0], one[1])
    above = jnp.where(odd, two, one)
    below = jnp.where(odd, one, two)
    rest = DEPTH * PLANE - MARGIN * PLANE
    total = core.astype(f32)
    total = total + jnp.pad(below.astype(f32), ((0, 0), (0, 0), (0, rest)))
    total = total + jnp.pad(above.astype(f32), ((0, 0), (0, 0), (rest, 0)))
    return jnp.transpose(total.astype(bf16), (1, 0, 2))


def solution(mesh):
    return jax.shard_map(
        shards,
        mesh=mesh,
        in_specs=(P(("slab", "work"), None), P(("slab", "work")), P(), P(), P(), P(), P()),
        out_specs=P(("slab", "work"), None, None),
        check_vma=False,
    )
```

```python
import functools

import jax
import jax.numpy as jnp
from jax import lax
from jax.experimental import pallas as pl
from jax.experimental.pallas import tpu as pltpu
from jax.sharding import PartitionSpec as P

SIDE = 32
DEPTH = 16
MARGIN = 4
EXTENT = 24
CHANNELS = 24
COARSE = 48
CLASSES = 3
OWNED = 2
HALF = EXTENT // 2
LANES = 256
PLANE = SIDE * SIDE
VROWS = 32
HROWS = 8 * CHANNELS
PROWS = 224
BIG = -1e30
ENDS = (6,)

f32 = jnp.float32
bf16 = jnp.bfloat16


def dot(a, b):
    return jnp.dot(a, b, preferred_element_type=f32)


def iota(shape, dim):
    return lax.broadcasted_iota(jnp.int32, shape, dim)


def along_x(x, sx, xx):
    x = [pltpu.roll(x[:, 128 * d : 128 * d + 128], (-sx) % 128, 1) for d in range(2)]
    return jnp.where(xx == (15 if sx > 0 else 0), 0.0, jnp.concatenate(x, axis=1))


def along_y(x, sy, yy):
    x = [pltpu.roll(x[:, 128 * d : 128 * d + 128], (-16 * sy) % 128, 1) for d in range(2)]
    zero = jnp.zeros_like(x[0])
    edge = yy[:, 0:128] == (7 if sy > 0 else 0)
    low = jnp.where(edge, x[1] if sy > 0 else zero, x[0])
    high = jnp.where(edge, zero if sy > 0 else x[0], x[1])
    return jnp.concatenate([low, high], axis=1)


def shifted(x, sy, sx, yy, xx):
    x = along_x(x, sx, xx) if sx else x
    return along_y(x, sy, yy) if sy else x


def swap_chunks(parts, low):
    out = []
    for j in range(4):
        halves = []
        for d in range(2):
            piece = [parts[2 * d + i][:, 128 * (j // 2) : 128 * (j // 2) + 128] for i in range(2)]
            if j % 2 == 0:
                halves.append(jnp.where(low, piece[0], pltpu.roll(piece[1], 64, 1)))
            else:
                halves.append(jnp.where(low, pltpu.roll(piece[0], 64, 1), piece[1]))
        out.append(jnp.concatenate(halves, axis=1))
    return out


def unet(*refs):
    hbm, (core, low_out, high_out), local = refs[:7], refs[7:10], refs[10:17]
    sems = refs[17]
    copies = [pltpu.make_async_copy(a, c, sems.at[k]) for k, (a, c) in enumerate(zip(hbm, local))]
    for copy in copies:
        copy.start()
    evaluate_bricks(copies, *local, core, low_out, high_out, *refs[18:])


def evaluate_bricks(
    copies, tissue, vol, w1, w2, wd, wup, wout, core, low_out, high_out,
    t1, b2, td, w1big, w2big, wd3, wo, vs, vz, hx, fs, ps, px, ys, gs, us, zs, rs,
):
    lane = iota((1, LANES), 1)
    yy, xx = lane >> 4, lane & 15
    low64 = iota((1, 128), 1) < 64

    rs[...] = jnp.zeros_like(rs)
    for b in range(OWNED):
        vz[b] = jnp.zeros((2, 26 * VROWS, 128), f32)
        hx[b, 0:HROWS] = jnp.zeros((HROWS, LANES), bf16)
        hx[b, 25 * HROWS : 26 * HROWS] = jnp.zeros((HROWS, LANES), bf16)
        ys[b, 0] = jnp.zeros((144, LANES), f32)
        ys[b, HALF + 1] = jnp.zeros((144, LANES), f32)
        for row, m in ((24, yy == 0), (25, yy == 15)):
            for d in range(2):
                vz[b, d, pl.ds(row, 26, stride=VROWS), :] = jnp.broadcast_to(
                    m[:, 128 * d : 128 * d + 128].astype(f32), (26, 128)
                )
    t1[...] = jnp.zeros_like(t1)
    b2[...] = jnp.zeros_like(b2)
    td[...] = jnp.zeros_like(td)
    for copy in copies:
        copy.wait()
    alive = tissue[0] + tissue[1]

    work = functools.partial(
        run, lane, yy, xx, low64, vol, w1, w2, wd, wup, wout, core, low_out, high_out,
        t1, b2, td, w1big, w2big, wd3, wo, vs, vz, hx, fs, ps, px, ys, gs, us, zs, rs,
    )

    @pl.when(alive == 2)
    def _():
        work([0, 1])

    @pl.when(alive == 1)
    def _():
        work([1 - tissue[0]])

    @pl.when(alive == 0)
    def _():
        for ref in (core, low_out, high_out):
            ref[...] = jnp.zeros_like(ref)


def run(
    lane, yy, xx, low64, vol, w1, w2, wd, wup, wout, core, low_out, high_out,
    t1, b2, td, w1big, w2big, wd3, wo, vs, vz, hx, fs, ps, px, ys, gs, us, zs, rs, bricks,
):
    for kz in range(3):
        for ky in range(3):
            at = kz * VROWS + ky * 4
            t1[at : at + 3, 0:CHANNELS] = w1[kz * 3 + ky].astype(f32)
    base1 = t1[...].T[0:CHANNELS]
    for pz in range(2):
        for ey in range(4):
            rows = []
            for ox in range(2):
                s = pz * VROWS + ey * 4 + ox
                m = pltpu.roll(base1, s, 1) if s else base1
                if ey in (0, 3):
                    m = jnp.where(lane[:, 0:128] == (24 if ey == 0 else 25), BIG, m)
                rows.append(m)
            at = (pz * 8 + ey * 2) * CHANNELS
            w1big[at : at + 48] = jnp.concatenate(rows, axis=0).astype(bf16)

    for ox in range(4):
        for kz in range(3):
            for ky in range(3):
                piece = [
                    w2[kz * 9 + ky * 3 + 2 - ox + dx].astype(f32)
                    if 0 <= 2 - ox + dx < 3
                    else jnp.zeros((CHANNELS, CHANNELS), f32)
                    for dx in range(2)
                ]
                at = kz * HROWS + ky * 48
                b2[ox, :, at : at + 48] = jnp.concatenate(piece, axis=1)
    for ox in range(4):
        base2 = b2[ox]
        for oz in range(2):
            rows = []
            for oy in range(2):
                s = oz * HROWS + oy * 48
                rows.append(pltpu.roll(base2, s, 1) if s else base2)
            at = (ox * 4 + oz * 2) * CHANNELS
            w2big[at : at + 48] = jnp.concatenate(rows, axis=0).astype(bf16)

    for kz in range(3):
        for k in range(9):
            td[kz, k * 24 : k * 24 + 24, 0:COARSE] = wd[kz * 9 + k].astype(f32)
    for kz in range(3):
        wd3[kz * COARSE : kz * COARSE + COARSE] = td[kz].T[0:COARSE, 0:PROWS].astype(bf16)

    ci = iota((CHANNELS, 192), 0)
    col = iota((CHANNELS, 192), 1)
    tiled = dot(wout[...], (col % 24 == ci).astype(bf16))
    r = iota((32, 192), 0)
    c = iota((32, 192), 1) // 24
    acc = jnp.zeros((32, 192), f32)
    for cls in range(CLASSES):
        acc = acc + jnp.where((r & 3) == cls, tiled[cls : cls + 1], 0.0)
    cell = ((r >> 3) & 1) * 4 + ((r >> 2) & 1) * 2 + (r >> 4)
    wo[...] = jnp.where(c == cell, acc, 0.0).astype(bf16)

    def source(l):
        p = l >> 6
        return ((l >> 4) & 3) * 64 + (p >> 1) * 32 + (l & 15) * 2 + (p & 1)

    sort = (iota((LANES, LANES), 0) == source(lane)).astype(bf16)
    unsort = (iota((LANES, LANES), 1) == source(iota((LANES, 1), 0))).astype(bf16)

    for z in range(EXTENT):
        for t in range(4):
            at = z * PLANE + t * LANES
            for d in range(2):
                vs[d, pl.ds(t * EXTENT + z, OWNED, stride=96), :] = vol[
                    :, at + 128 * d : at + 128 * d + 128
                ].astype(f32)
    if len(bricks) == OWNED:
        cells = [vs[d] for d in range(2)]
    else:
        cells = [vs[d, pl.ds(pl.multiple_of(bricks[0] * 96, 96), 96), :] for d in range(2)]
    sorted_cells = dot(jnp.concatenate(cells, axis=1).astype(bf16), sort)
    for b in range(len(bricks)):
        parts = [sorted_cells[b * 96 + t * 24 : b * 96 + t * 24 + 24] for t in range(4)]
        parities = swap_chunks(parts, low64)
        for p in range(4):
            for sy in (-1, 0, 1):
                for sx in ((0, 1) if p & 1 == 0 else (-1, 0)):
                    row = (2 * sy + (p >> 1) + 2) * 4 + 2 * sx + (p & 1) + 1
                    near = shifted(parities[p], sy, sx, yy, xx)
                    for d in range(2):
                        vz[b, d, pl.ds(VROWS + row, EXTENT, stride=VROWS), :] = near[
                            :, 128 * d : 128 * d + 128
                        ]

    def first(j):
        b, i = j // HALF, j % HALF
        at = i * (2 * VROWS)
        near = [vz[b, d, pl.ds(at, 4 * VROWS), :] for d in range(2)]
        near = jnp.concatenate(near, axis=1).astype(bf16)
        out = jnp.maximum(dot(w1big[...], near), 0.0).astype(bf16)
        to = i * (2 * HROWS) + HROWS
        hx[b, pl.ds(to, 2 * HROWS), :] = out

    def second(j):
        b, i = j // HALF, j % HALF
        at = i * (2 * HROWS)
        out = dot(w2big[...], hx[b, pl.ds(at, 4 * HROWS), :])
        left = out[96:192] + along_x(out[288:384], -1, xx)
        right = out[192:288] + along_x(out[0:96], 1, xx)
        fine = jnp.maximum(jnp.concatenate([left, right], axis=0), 0.0)
        fs[b, i] = fine.astype(bf16)
        ps[j] = functools.reduce(jnp.maximum, [fine[c * 24 : c * 24 + 24] for c in range(8)])

    def spread(j):
        p = ps[j]
        near = [shifted(p, sy, sx, yy, xx) for sy in (-1, 0, 1) for sx in (-1, 0, 1)]
        near = jnp.concatenate(near + [jnp.zeros((8, LANES), f32)], axis=0).astype(bf16)
        px[j] = near

    def coarse(j):
        b, i = j // HALF, j % HALF
        ys[b, i + 1] = dot(wd3[...], px[j])

    def gather(j):
        b, i = j // HALF, j % HALF
        g = ys[b, i, 0:48] + ys[b, i + 1, 48:96] + ys[b, i + 2, 96:144]
        gs[j] = jnp.maximum(g, 0.0).astype(bf16)

    def lift(j):
        us[j] = dot(wup[...], gs[j])

    def mix(j):
        b, i = j // HALF, j % HALF
        fine = fs[b, i].astype(f32).reshape(8, CHANNELS, LANES)
        z = jnp.maximum(fine + us[j][None], 0.0).reshape(8 * CHANNELS, LANES)
        zs[j] = z.astype(bf16)

    def project(j):
        b, i = j // HALF, j % HALF
        pred = jax.nn.sigmoid(dot(wo[...], zs[j]))
        for p in range(4):
            for d in range(2):
                rs[p, d, pl.ds(i * 16 + bricks[b], 8, stride=2), :] = pred[
                    p * 8 : p * 8 + 8, 128 * d : 128 * d + 128
                ]

    def emit(first_layer, layers):
        at = first_layer * 16
        parts = [
            jnp.concatenate([rs[p, d, at : at + layers * 16] for d in range(2)], axis=1)
            for p in range(4)
        ]
        chunks = swap_chunks(parts, low64)
        for t in range(4):
            rows = dot(chunks[t].astype(bf16), unsort)
            for z in range(2 * first_layer, 2 * (first_layer + layers)):
                if z < MARGIN:
                    to, ref = z, low_out
                elif z < MARGIN + DEPTH:
                    to, ref = z - MARGIN, core
                else:
                    to, ref = z - MARGIN - DEPTH, high_out
                to = to * PLANE + t * LANES
                for cls in range(CLASSES):
                    r = (z - 2 * first_layer) * 8 + cls * 2
                    ref[cls, :, to : to + LANES] = rows[r : r + 2].astype(bf16)

    start = 0
    for step in range(-2, HALF + 4):
        for stage, lag in (
            (second, 0), (coarse, -1), (lift, -3), (project, -4),
            (first, 2), (mix, -3), (gather, -2), (spread, 0),
        ):
            if 0 <= step + lag < HALF:
                for b in range(len(bricks)):
                    stage(b * HALF + step + lag)
        for end in ENDS:
            if step == end + 3:
                emit(start, end - start)
                start = end
    if start < HALF:
        emit(start, HALF - start)


VMEM = pl.BlockSpec(memory_space=pltpu.VMEM)


def evaluate(volume, tissue, w_first, w_second, w_down, w_up, w_out):
    w1 = jnp.transpose(w_first, (1, 2, 3, 4, 0)).reshape(9, 3, CHANNELS)
    w2 = jnp.transpose(w_second, (2, 3, 4, 0, 1)).reshape(27, CHANNELS, CHANNELS)
    wd = jnp.transpose(w_down, (2, 3, 4, 1, 0)).reshape(27, CHANNELS, COARSE)
    edge = jax.ShapeDtypeStruct((CLASSES, OWNED, MARGIN * PLANE), bf16)
    arrays = [pltpu.with_memory_space_constraint(a, pltpu.HBM) for a in (tissue, volume, w1, w2, wd, w_up, w_out)]
    return pl.pallas_call(
        unet,
        out_shape=(jax.ShapeDtypeStruct((CLASSES, OWNED, DEPTH * PLANE), bf16), edge, edge),
        in_specs=[pl.BlockSpec(memory_space=pltpu.HBM)] * 7,
        out_specs=(VMEM,) * 3,
        scratch_shapes=[pltpu.SMEM(tissue.shape, tissue.dtype)]
        + [pltpu.VMEM(a.shape, a.dtype) for a in arrays[1:]]
        + [
            pltpu.SemaphoreType.DMA((7,)),
            pltpu.VMEM((128, 128), f32),
            pltpu.VMEM((4, CHANNELS, 4 * HROWS), f32),
            pltpu.VMEM((3, 256, 128), f32),
            pltpu.VMEM((2 * HROWS, 4 * VROWS), bf16),
            pltpu.VMEM((384, 4 * HROWS), bf16),
            pltpu.VMEM((144, PROWS), bf16),
            pltpu.VMEM((32, 192), bf16),
            pltpu.VMEM((2, 192, 128), f32),
            pltpu.VMEM((OWNED, 2, 26 * VROWS, 128), f32),
            pltpu.VMEM((OWNED, 26 * HROWS, LANES), bf16),
            pltpu.VMEM((OWNED, HALF, 192, LANES), bf16),
            pltpu.VMEM((OWNED * HALF, CHANNELS, LANES), f32),
            pltpu.VMEM((OWNED * HALF, PROWS, LANES), bf16),
            pltpu.VMEM((OWNED, HALF + 2, 144, LANES), f32),
            pltpu.VMEM((OWNED * HALF, COARSE, LANES), bf16),
            pltpu.VMEM((OWNED * HALF, CHANNELS, LANES), f32),
            pltpu.VMEM((OWNED * HALF, 8 * CHANNELS, LANES), bf16),
            pltpu.VMEM((4, 2, EXTENT * 8, 128), f32),
        ],
        compiler_params=pltpu.CompilerParams(vmem_limit_bytes=48 << 20),
    )(*arrays)


def shards(volume, tissue, w_first, w_second, w_down, w_up, w_out):
    core, low, high = evaluate(volume, tissue, w_first, w_second, w_down, w_up, w_out)
    slabs = lax.axis_size("slab")
    me = lax.axis_index("slab")
    odd = (me % 2) == 1
    across = [(i, i + 1) for i in range(1, slabs - 1, 2)] + [(i + 1, i) for i in range(1, slabs - 1, 2)]
    chip = [[i, i + 1] for i in range(0, slabs, 2)]
    two = lax.ppermute(jnp.where(odd, high, low), "slab", across)
    one = lax.all_gather(jnp.where(odd, low, high), "slab", axis_index_groups=chip)
    one = jnp.where(odd, one[0], one[1])
    above = jnp.where(odd, two, one)
    below = jnp.where(odd, one, two)
    rest = DEPTH * PLANE - MARGIN * PLANE
    total = core.astype(f32)
    total = total + jnp.pad(below.astype(f32), ((0, 0), (0, 0), (0, rest)))
    total = total + jnp.pad(above.astype(f32), ((0, 0), (0, 0), (rest, 0)))
    return jnp.transpose(total.astype(bf16), (1, 0, 2))


def solution(mesh):
    return jax.shard_map(
        shards,
        mesh=mesh,
        in_specs=(P(("slab", "work"), None), P(("slab", "work")), P(), P(), P(), P(), P()),
        out_specs=P(("slab", "work"), None, None),
        check_vma=False,
    )
```

```python
import functools

import jax
import jax.numpy as jnp
from jax import lax
from jax.experimental import pallas as pl
from jax.experimental.pallas import tpu as pltpu
from jax.sharding import PartitionSpec as P

SIDE = 32
DEPTH = 16
MARGIN = 4
EXTENT = 24
CHANNELS = 24
COARSE = 48
CLASSES = 3
OWNED = 2
HALF = EXTENT // 2
LANES = 256
PLANE = SIDE * SIDE
VROWS = 32
HROWS = 8 * CHANNELS
PROWS = 224
BIG = -1e30

f32 = jnp.float32
bf16 = jnp.bfloat16


def dot(a, b):
    return jnp.dot(a, b, preferred_element_type=f32)


def iota(shape, dim):
    return lax.broadcasted_iota(jnp.int32, shape, dim)


def along_x(x, sx, xx):
    x = [pltpu.roll(x[:, 128 * d : 128 * d + 128], (-sx) % 128, 1) for d in range(2)]
    return jnp.where(xx == (15 if sx > 0 else 0), 0.0, jnp.concatenate(x, axis=1))


def along_y(x, sy, yy):
    x = [pltpu.roll(x[:, 128 * d : 128 * d + 128], (-16 * sy) % 128, 1) for d in range(2)]
    zero = jnp.zeros_like(x[0])
    edge = yy[:, 0:128] == (7 if sy > 0 else 0)
    low = jnp.where(edge, x[1] if sy > 0 else zero, x[0])
    high = jnp.where(edge, zero if sy > 0 else x[0], x[1])
    return jnp.concatenate([low, high], axis=1)


def shifted(x, sy, sx, yy, xx):
    x = along_x(x, sx, xx) if sx else x
    return along_y(x, sy, yy) if sy else x


def swap_chunks(parts, low):
    out = []
    for j in range(4):
        halves = []
        for d in range(2):
            piece = [parts[2 * d + i][:, 128 * (j // 2) : 128 * (j // 2) + 128] for i in range(2)]
            if j % 2 == 0:
                halves.append(jnp.where(low, piece[0], pltpu.roll(piece[1], 64, 1)))
            else:
                halves.append(jnp.where(low, pltpu.roll(piece[0], 64, 1), piece[1]))
        out.append(jnp.concatenate(halves, axis=1))
    return out


def unet(*refs):
    hbm, (core, low_out, high_out), local = refs[:7], refs[7:10], refs[10:17]
    sems = refs[17]
    copies = [pltpu.make_async_copy(a, c, sems.at[k]) for k, (a, c) in enumerate(zip(hbm, local))]
    for copy in copies:
        copy.start()
    evaluate_bricks(copies, *local, core, low_out, high_out, *refs[18:])


def evaluate_bricks(
    copies, tissue, vol, w1, w2, wd, wup, wout, core, low_out, high_out,
    t1, b2, td, w1big, w2big, wd3, wo, vs, vz, hx, fs, ps, px, ys, gs, us, zs, rs,
):
    lane = iota((1, LANES), 1)
    yy, xx = lane >> 4, lane & 15
    low64 = iota((1, 128), 1) < 64

    rs[...] = jnp.zeros_like(rs)
    for b in range(OWNED):
        vz[b] = jnp.zeros((2, 26 * VROWS, 128), f32)
        hx[b, 0:HROWS] = jnp.zeros((HROWS, LANES), bf16)
        hx[b, 25 * HROWS : 26 * HROWS] = jnp.zeros((HROWS, LANES), bf16)
        ys[b, 0] = jnp.zeros((144, LANES), f32)
        ys[b, HALF + 1] = jnp.zeros((144, LANES), f32)
        for row, m in ((24, yy == 0), (25, yy == 15)):
            for d in range(2):
                vz[b, d, pl.ds(row, 26, stride=VROWS), :] = jnp.broadcast_to(
                    m[:, 128 * d : 128 * d + 128].astype(f32), (26, 128)
                )
    t1[...] = jnp.zeros_like(t1)
    b2[...] = jnp.zeros_like(b2)
    td[...] = jnp.zeros_like(td)
    for copy in copies:
        copy.wait()
    alive = tissue[0] + tissue[1]

    work = functools.partial(
        run, lane, yy, xx, low64, vol, w1, w2, wd, wup, wout, core, low_out, high_out,
        t1, b2, td, w1big, w2big, wd3, wo, vs, vz, hx, fs, ps, px, ys, gs, us, zs, rs,
    )

    @pl.when(alive == 2)
    def _():
        work([0, 1])

    @pl.when(alive == 1)
    def _():
        work([1 - tissue[0]])

    @pl.when(alive == 0)
    def _():
        for ref in (core, low_out, high_out):
            ref[...] = jnp.zeros_like(ref)


def run(
    lane, yy, xx, low64, vol, w1, w2, wd, wup, wout, core, low_out, high_out,
    t1, b2, td, w1big, w2big, wd3, wo, vs, vz, hx, fs, ps, px, ys, gs, us, zs, rs, bricks,
):
    for kz in range(3):
        for ky in range(3):
            at = kz * VROWS + ky * 4
            t1[at : at + 3, 0:CHANNELS] = w1[kz * 3 + ky].astype(f32)
    base1 = t1[...].T[0:CHANNELS]
    for pz in range(2):
        for ey in range(4):
            rows = []
            for ox in range(2):
                s = pz * VROWS + ey * 4 + ox
                m = pltpu.roll(base1, s, 1) if s else base1
                if ey in (0, 3):
                    m = jnp.where(lane[:, 0:128] == (24 if ey == 0 else 25), BIG, m)
                rows.append(m)
            at = (pz * 8 + ey * 2) * CHANNELS
            w1big[at : at + 48] = jnp.concatenate(rows, axis=0).astype(bf16)

    for ox in range(4):
        for kz in range(3):
            for ky in range(3):
                piece = [
                    w2[kz * 9 + ky * 3 + 2 - ox + dx].astype(f32)
                    if 0 <= 2 - ox + dx < 3
                    else jnp.zeros((CHANNELS, CHANNELS), f32)
                    for dx in range(2)
                ]
                at = kz * HROWS + ky * 48
                b2[ox, :, at : at + 48] = jnp.concatenate(piece, axis=1)
    for ox in range(4):
        base2 = b2[ox]
        for oz in range(2):
            rows = []
            for oy in range(2):
                s = oz * HROWS + oy * 48
                rows.append(pltpu.roll(base2, s, 1) if s else base2)
            at = (ox * 4 + oz * 2) * CHANNELS
            w2big[at : at + 48] = jnp.concatenate(rows, axis=0).astype(bf16)

    for kz in range(3):
        for k in range(9):
            td[kz, k * 24 : k * 24 + 24, 0:COARSE] = wd[kz * 9 + k].astype(f32)
    for kz in range(3):
        wd3[kz * COARSE : kz * COARSE + COARSE] = td[kz].T[0:COARSE, 0:PROWS].astype(bf16)

    ci = iota((CHANNELS, 192), 0)
    col = iota((CHANNELS, 192), 1)
    tiled = dot(wout[...], (col % 24 == ci).astype(bf16))
    r = iota((32, 192), 0)
    c = iota((32, 192), 1) // 24
    acc = jnp.zeros((32, 192), f32)
    for cls in range(CLASSES):
        acc = acc + jnp.where((r & 3) == cls, tiled[cls : cls + 1], 0.0)
    cell = ((r >> 3) & 1) * 4 + ((r >> 2) & 1) * 2 + (r >> 4)
    wo[...] = jnp.where(c == cell, acc, 0.0).astype(bf16)

    def source(l):
        p = l >> 6
        return ((l >> 4) & 3) * 64 + (p >> 1) * 32 + (l & 15) * 2 + (p & 1)

    sort = (iota((LANES, LANES), 0) == source(lane)).astype(bf16)
    unsort = (iota((LANES, LANES), 1) == source(iota((LANES, 1), 0))).astype(bf16)

    for z in range(EXTENT):
        for t in range(4):
            at = z * PLANE + t * LANES
            for d in range(2):
                vs[d, pl.ds(t * EXTENT + z, OWNED, stride=96), :] = vol[
                    :, at + 128 * d : at + 128 * d + 128
                ].astype(f32)
    if len(bricks) == OWNED:
        cells = [vs[d] for d in range(2)]
    else:
        cells = [vs[d, pl.ds(pl.multiple_of(bricks[0] * 96, 96), 96), :] for d in range(2)]
    sorted_cells = dot(jnp.concatenate(cells, axis=1).astype(bf16), sort)
    for b in range(len(bricks)):
        parts = [sorted_cells[b * 96 + t * 24 : b * 96 + t * 24 + 24] for t in range(4)]
        parities = swap_chunks(parts, low64)
        for p in range(4):
            for sy in (-1, 0, 1):
                for sx in ((0, 1) if p & 1 == 0 else (-1, 0)):
                    row = (2 * sy + (p >> 1) + 2) * 4 + 2 * sx + (p & 1) + 1
                    near = shifted(parities[p], sy, sx, yy, xx)
                    for d in range(2):
                        vz[b, d, pl.ds(VROWS + row, EXTENT, stride=VROWS), :] = near[
                            :, 128 * d : 128 * d + 128
                        ]

    def first(j):
        b, i = j // HALF, j % HALF
        at = i * (2 * VROWS)
        near = [vz[b, d, pl.ds(at, 4 * VROWS), :] for d in range(2)]
        near = jnp.concatenate(near, axis=1).astype(bf16)
        out = jnp.maximum(dot(w1big[...], near), 0.0).astype(bf16)
        to = i * (2 * HROWS) + HROWS
        hx[b, pl.ds(to, 2 * HROWS), :] = out

    def second(j):
        b, i = j // HALF, j % HALF
        at = i * (2 * HROWS)
        out = dot(w2big[...], hx[b, pl.ds(at, 4 * HROWS), :])
        left = out[96:192] + along_x(out[288:384], -1, xx)
        right = out[192:288] + along_x(out[0:96], 1, xx)
        fine = jnp.maximum(jnp.concatenate([left, right], axis=0), 0.0)
        fs[b, i] = fine.astype(bf16)
        ps[j] = functools.reduce(jnp.maximum, [fine[c * 24 : c * 24 + 24] for c in range(8)])

    def spread(j):
        p = ps[j]
        near = [shifted(p, sy, sx, yy, xx) for sy in (-1, 0, 1) for sx in (-1, 0, 1)]
        near = jnp.concatenate(near + [jnp.zeros((8, LANES), f32)], axis=0).astype(bf16)
        px[j] = near

    def coarse(j):
        b, i = j // HALF, j % HALF
        ys[b, i + 1] = dot(wd3[...], px[j])

    def gather(j):
        b, i = j // HALF, j % HALF
        g = ys[b, i, 0:48] + ys[b, i + 1, 48:96] + ys[b, i + 2, 96:144]
        gs[j] = jnp.maximum(g, 0.0).astype(bf16)

    def lift(j):
        us[j] = dot(wup[...], gs[j])

    def mix(j):
        b, i = j // HALF, j % HALF
        fine = fs[b, i].astype(f32).reshape(8, CHANNELS, LANES)
        z = jnp.maximum(fine + us[j][None], 0.0).reshape(8 * CHANNELS, LANES)
        zs[j] = z.astype(bf16)

    def project(j):
        b, i = j // HALF, j % HALF
        pred = jax.nn.sigmoid(dot(wo[...], zs[j]))
        for p in range(4):
            for d in range(2):
                rs[p, d, pl.ds(i * 16 + bricks[b], 8, stride=2), :] = pred[
                    p * 8 : p * 8 + 8, 128 * d : 128 * d + 128
                ]

    def emit():
        parts = [jnp.concatenate([rs[p, d] for d in range(2)], axis=1) for p in range(4)]
        chunks = swap_chunks(parts, low64)
        for t in range(4):
            rows = dot(chunks[t].astype(bf16), unsort)
            for z in range(EXTENT):
                if z < MARGIN:
                    to, ref = z, low_out
                elif z < MARGIN + DEPTH:
                    to, ref = z - MARGIN, core
                else:
                    to, ref = z - MARGIN - DEPTH, high_out
                to = to * PLANE + t * LANES
                for cls in range(CLASSES):
                    piece = rows[z * 8 + cls * 2 : z * 8 + cls * 2 + 2].astype(bf16)
                    ref[cls, :, to : to + LANES] = piece

    half = HALF // 2
    for step in range(-2, half + 4):
        for stage, lag in (
            (second, 0), (first, 2), (coarse, -1), (lift, -3), (project, -4),
            (mix, -3), (gather, -2), (spread, 0),
        ):
            k = step + lag
            if 0 <= k < half:
                for b in range(len(bricks)):
                    for i in (k, HALF - 1 - k):
                        stage(b * HALF + i)
    emit()


VMEM = pl.BlockSpec(memory_space=pltpu.VMEM)


def evaluate(volume, tissue, w_first, w_second, w_down, w_up, w_out):
    w1 = jnp.transpose(w_first, (1, 2, 3, 4, 0)).reshape(9, 3, CHANNELS)
    w2 = jnp.transpose(w_second, (2, 3, 4, 0, 1)).reshape(27, CHANNELS, CHANNELS)
    wd = jnp.transpose(w_down, (2, 3, 4, 1, 0)).reshape(27, CHANNELS, COARSE)
    edge = jax.ShapeDtypeStruct((CLASSES, OWNED, MARGIN * PLANE), bf16)
    arrays = [pltpu.with_memory_space_constraint(a, pltpu.HBM) for a in (tissue, volume, w1, w2, wd, w_up, w_out)]
    return pl.pallas_call(
        unet,
        out_shape=(jax.ShapeDtypeStruct((CLASSES, OWNED, DEPTH * PLANE), bf16), edge, edge),
        in_specs=[pl.BlockSpec(memory_space=pltpu.HBM)] * 7,
        out_specs=(VMEM,) * 3,
        scratch_shapes=[pltpu.SMEM(tissue.shape, tissue.dtype)]
        + [pltpu.VMEM(a.shape, a.dtype) for a in arrays[1:]]
        + [
            pltpu.SemaphoreType.DMA((7,)),
            pltpu.VMEM((128, 128), f32),
            pltpu.VMEM((4, CHANNELS, 4 * HROWS), f32),
            pltpu.VMEM((3, 256, 128), f32),
            pltpu.VMEM((2 * HROWS, 4 * VROWS), bf16),
            pltpu.VMEM((384, 4 * HROWS), bf16),
            pltpu.VMEM((144, PROWS), bf16),
            pltpu.VMEM((32, 192), bf16),
            pltpu.VMEM((2, 192, 128), f32),
            pltpu.VMEM((OWNED, 2, 26 * VROWS, 128), f32),
            pltpu.VMEM((OWNED, 26 * HROWS, LANES), bf16),
            pltpu.VMEM((OWNED, HALF, 192, LANES), bf16),
            pltpu.VMEM((OWNED * HALF, CHANNELS, LANES), f32),
            pltpu.VMEM((OWNED * HALF, PROWS, LANES), bf16),
            pltpu.VMEM((OWNED, HALF + 2, 144, LANES), f32),
            pltpu.VMEM((OWNED * HALF, COARSE, LANES), bf16),
            pltpu.VMEM((OWNED * HALF, CHANNELS, LANES), f32),
            pltpu.VMEM((OWNED * HALF, 8 * CHANNELS, LANES), bf16),
            pltpu.VMEM((4, 2, EXTENT * 8, 128), f32),
        ],
        compiler_params=pltpu.CompilerParams(vmem_limit_bytes=48 << 20),
    )(*arrays)


def shards(volume, tissue, w_first, w_second, w_down, w_up, w_out):
    core, low, high = evaluate(volume, tissue, w_first, w_second, w_down, w_up, w_out)
    slabs = lax.axis_size("slab")
    me = lax.axis_index("slab")
    odd = (me % 2) == 1
    across = [(i, i + 1) for i in range(1, slabs - 1, 2)] + [(i + 1, i) for i in range(1, slabs - 1, 2)]
    chip = [[i, i + 1] for i in range(0, slabs, 2)]
    two = lax.ppermute(jnp.where(odd, high, low), "slab", across)
    one = lax.all_gather(jnp.where(odd, low, high), "slab", axis_index_groups=chip)
    one = jnp.where(odd, one[0], one[1])
    above = jnp.where(odd, two, one)
    below = jnp.where(odd, one, two)
    rest = DEPTH * PLANE - MARGIN * PLANE
    total = core.astype(f32)
    total = total + jnp.pad(below.astype(f32), ((0, 0), (0, 0), (0, rest)))
    total = total + jnp.pad(above.astype(f32), ((0, 0), (0, 0), (rest, 0)))
    return jnp.transpose(total.astype(bf16), (1, 0, 2))


def solution(mesh):
    return jax.shard_map(
        shards,
        mesh=mesh,
        in_specs=(P(("slab", "work"), None), P(("slab", "work")), P(), P(), P(), P(), P()),
        out_specs=P(("slab", "work"), None, None),
        check_vma=False,
    )
```

```python
import functools

import jax
import jax.numpy as jnp
from jax import lax
from jax.experimental import pallas as pl
from jax.experimental.pallas import tpu as pltpu
from jax.sharding import PartitionSpec as P

SIDE = 32
DEPTH = 16
MARGIN = 4
EXTENT = 24
CHANNELS = 24
COARSE = 48
CLASSES = 3
OWNED = 2
HALF = EXTENT // 2
LANES = 256
PLANE = SIDE * SIDE
VROWS = 32
HROWS = 8 * CHANNELS
PROWS = 224
BIG = -1e30

f32 = jnp.float32
bf16 = jnp.bfloat16


def dot(a, b):
    return jnp.dot(a, b, preferred_element_type=f32)


def iota(shape, dim):
    return lax.broadcasted_iota(jnp.int32, shape, dim)


def along_x(x, sx, xx):
    x = [pltpu.roll(x[:, 128 * d : 128 * d + 128], (-sx) % 128, 1) for d in range(2)]
    return jnp.where(xx == (15 if sx > 0 else 0), 0.0, jnp.concatenate(x, axis=1))


def along_y(x, sy, yy):
    x = [pltpu.roll(x[:, 128 * d : 128 * d + 128], (-16 * sy) % 128, 1) for d in range(2)]
    zero = jnp.zeros_like(x[0])
    edge = yy[:, 0:128] == (7 if sy > 0 else 0)
    low = jnp.where(edge, x[1] if sy > 0 else zero, x[0])
    high = jnp.where(edge, zero if sy > 0 else x[0], x[1])
    return jnp.concatenate([low, high], axis=1)


def shifted(x, sy, sx, yy, xx):
    x = along_x(x, sx, xx) if sx else x
    return along_y(x, sy, yy) if sy else x


def swap_chunks(parts, low):
    out = []
    for j in range(4):
        halves = []
        for d in range(2):
            piece = [parts[2 * d + i][:, 128 * (j // 2) : 128 * (j // 2) + 128] for i in range(2)]
            if j % 2 == 0:
                halves.append(jnp.where(low, piece[0], pltpu.roll(piece[1], 64, 1)))
            else:
                halves.append(jnp.where(low, pltpu.roll(piece[0], 64, 1), piece[1]))
        out.append(jnp.concatenate(halves, axis=1))
    return out


def unet(*refs):
    hbm, (core, low_out, high_out), local = refs[:7], refs[7:10], refs[10:17]
    sems = refs[17]
    copies = [pltpu.make_async_copy(a, c, sems.at[k]) for k, (a, c) in enumerate(zip(hbm, local))]
    for copy in copies:
        copy.start()
    evaluate_bricks(copies, *local, core, low_out, high_out, *refs[18:])


def evaluate_bricks(
    copies, tissue, vol, w1, w2, wd, wup, wout, core, low_out, high_out,
    t1, b2, td, w1big, w2big, wd3, wo, vs, vz, hx, fs, ps, px, ys, gs, us, zs, rs,
):
    lane = iota((1, LANES), 1)
    yy, xx = lane >> 4, lane & 15
    low64 = iota((1, 128), 1) < 64

    rs[...] = jnp.zeros_like(rs)
    for b in range(OWNED):
        vz[b] = jnp.zeros((2, 26 * VROWS, 128), f32)
        hx[b, 0:HROWS] = jnp.zeros((HROWS, LANES), bf16)
        hx[b, 25 * HROWS : 26 * HROWS] = jnp.zeros((HROWS, LANES), bf16)
        ys[b, 0] = jnp.zeros((144, LANES), f32)
        ys[b, HALF + 1] = jnp.zeros((144, LANES), f32)
        for row, m in ((24, yy == 0), (25, yy == 15)):
            for d in range(2):
                vz[b, d, pl.ds(row, 26, stride=VROWS), :] = jnp.broadcast_to(
                    m[:, 128 * d : 128 * d + 128].astype(f32), (26, 128)
                )
    t1[...] = jnp.zeros_like(t1)
    b2[...] = jnp.zeros_like(b2)
    td[...] = jnp.zeros_like(td)
    for copy in copies:
        copy.wait()
    alive = tissue[0] + tissue[1]

    work = functools.partial(
        run, lane, yy, xx, low64, vol, w1, w2, wd, wup, wout, core, low_out, high_out,
        t1, b2, td, w1big, w2big, wd3, wo, vs, vz, hx, fs, ps, px, ys, gs, us, zs, rs,
    )

    @pl.when(alive == 2)
    def _():
        work([0, 1])

    @pl.when(alive == 1)
    def _():
        work([1 - tissue[0]])

    @pl.when(alive == 0)
    def _():
        for ref in (core, low_out, high_out):
            ref[...] = jnp.zeros_like(ref)


def run(
    lane, yy, xx, low64, vol, w1, w2, wd, wup, wout, core, low_out, high_out,
    t1, b2, td, w1big, w2big, wd3, wo, vs, vz, hx, fs, ps, px, ys, gs, us, zs, rs, bricks,
):
    for kz in range(3):
        for ky in range(3):
            at = kz * VROWS + ky * 4
            t1[at : at + 3, 0:CHANNELS] = w1[kz * 3 + ky].astype(f32)
    base1 = t1[...].T[0:CHANNELS]
    for pz in range(2):
        for ey in range(4):
            rows = []
            for ox in range(2):
                s = pz * VROWS + ey * 4 + ox
                m = pltpu.roll(base1, s, 1) if s else base1
                if ey in (0, 3):
                    m = jnp.where(lane[:, 0:128] == (24 if ey == 0 else 25), BIG, m)
                rows.append(m)
            at = (pz * 8 + ey * 2) * CHANNELS
            w1big[at : at + 48] = jnp.concatenate(rows, axis=0).astype(bf16)

    for ox in range(4):
        for kz in range(3):
            for ky in range(3):
                piece = [
                    w2[kz * 9 + ky * 3 + 2 - ox + dx].astype(f32)
                    if 0 <= 2 - ox + dx < 3
                    else jnp.zeros((CHANNELS, CHANNELS), f32)
                    for dx in range(2)
                ]
                at = kz * HROWS + ky * 48
                b2[ox, :, at : at + 48] = jnp.concatenate(piece, axis=1)
    for ox in range(4):
        base2 = b2[ox]
        for oz in range(2):
            rows = []
            for oy in range(2):
                s = oz * HROWS + oy * 48
                rows.append(pltpu.roll(base2, s, 1) if s else base2)
            at = (ox * 4 + oz * 2) * CHANNELS
            w2big[at : at + 48] = jnp.concatenate(rows, axis=0).astype(bf16)

    for kz in range(3):
        for k in range(9):
            td[kz, k * 24 : k * 24 + 24, 0:COARSE] = wd[kz * 9 + k].astype(f32)
    for kz in range(3):
        wd3[kz * COARSE : kz * COARSE + COARSE] = td[kz].T[0:COARSE, 0:PROWS].astype(bf16)

    ci = iota((CHANNELS, 192), 0)
    col = iota((CHANNELS, 192), 1)
    tiled = dot(wout[...], (col % 24 == ci).astype(bf16))
    r = iota((32, 192), 0)
    c = iota((32, 192), 1) // 24
    acc = jnp.zeros((32, 192), f32)
    for cls in range(CLASSES):
        acc = acc + jnp.where((r & 3) == cls, tiled[cls : cls + 1], 0.0)
    cell = ((r >> 3) & 1) * 4 + ((r >> 2) & 1) * 2 + (r >> 4)
    wo[...] = jnp.where(c == cell, acc, 0.0).astype(bf16)

    def source(l):
        p = l >> 6
        return ((l >> 4) & 3) * 64 + (p >> 1) * 32 + (l & 15) * 2 + (p & 1)

    sort = (iota((LANES, LANES), 0) == source(lane)).astype(bf16)
    unsort = (iota((LANES, LANES), 1) == source(iota((LANES, 1), 0))).astype(bf16)

    for z in range(EXTENT):
        for t in range(4):
            at = z * PLANE + t * LANES
            for d in range(2):
                vs[d, pl.ds(t * EXTENT + z, OWNED, stride=96), :] = vol[
                    :, at + 128 * d : at + 128 * d + 128
                ].astype(f32)
    if len(bricks) == OWNED:
        cells = [vs[d] for d in range(2)]
    else:
        cells = [vs[d, pl.ds(pl.multiple_of(bricks[0] * 96, 96), 96), :] for d in range(2)]
    sorted_cells = dot(jnp.concatenate(cells, axis=1).astype(bf16), sort)
    for b in range(len(bricks)):
        parts = [sorted_cells[b * 96 + t * 24 : b * 96 + t * 24 + 24] for t in range(4)]
        parities = swap_chunks(parts, low64)
        for p in range(4):
            for sy in (-1, 0, 1):
                for sx in ((0, 1) if p & 1 == 0 else (-1, 0)):
                    row = (2 * sy + (p >> 1) + 2) * 4 + 2 * sx + (p & 1) + 1
                    near = shifted(parities[p], sy, sx, yy, xx)
                    for d in range(2):
                        vz[b, d, pl.ds(VROWS + row, EXTENT, stride=VROWS), :] = near[
                            :, 128 * d : 128 * d + 128
                        ]

    def first(j):
        b, i = j // HALF, j % HALF
        at = i * (2 * VROWS)
        near = [vz[b, d, pl.ds(at, 4 * VROWS), :] for d in range(2)]
        near = jnp.concatenate(near, axis=1).astype(bf16)
        out = jnp.maximum(dot(w1big[...], near), 0.0).astype(bf16)
        to = i * (2 * HROWS) + HROWS
        hx[b, pl.ds(to, 2 * HROWS), :] = out

    def second(j):
        b, i = j // HALF, j % HALF
        at = i * (2 * HROWS)
        out = dot(w2big[...], hx[b, pl.ds(at, 4 * HROWS), :])
        left = out[96:192] + along_x(out[288:384], -1, xx)
        right = out[192:288] + along_x(out[0:96], 1, xx)
        fine = jnp.maximum(jnp.concatenate([left, right], axis=0), 0.0)
        fs[b, i] = fine.astype(bf16)
        ps[j] = functools.reduce(jnp.maximum, [fine[c * 24 : c * 24 + 24] for c in range(8)])

    def spread(j):
        p = ps[j]
        near = [shifted(p, sy, sx, yy, xx) for sy in (-1, 0, 1) for sx in (-1, 0, 1)]
        near = jnp.concatenate(near + [jnp.zeros((8, LANES), f32)], axis=0).astype(bf16)
        px[j] = near

    def coarse(j):
        b, i = j // HALF, j % HALF
        ys[b, i + 1] = dot(wd3[...], px[j])

    def gather(j):
        b, i = j // HALF, j % HALF
        g = ys[b, i, 0:48] + ys[b, i + 1, 48:96] + ys[b, i + 2, 96:144]
        gs[j] = jnp.maximum(g, 0.0).astype(bf16)

    def lift(j):
        us[j] = dot(wup[...], gs[j])

    def mix(j):
        b, i = j // HALF, j % HALF
        fine = fs[b, i].astype(f32).reshape(8, CHANNELS, LANES)
        z = jnp.maximum(fine + us[j][None], 0.0).reshape(8 * CHANNELS, LANES)
        zs[j] = z.astype(bf16)

    def project(j):
        b, i = j // HALF, j % HALF
        pred = jax.nn.sigmoid(dot(wo[...], zs[j]))
        for p in range(4):
            for d in range(2):
                rs[p, d, pl.ds(i * 16 + bricks[b], 8, stride=2), :] = pred[
                    p * 8 : p * 8 + 8, 128 * d : 128 * d + 128
                ]

    def emit():
        parts = [jnp.concatenate([rs[p, d] for d in range(2)], axis=1) for p in range(4)]
        chunks = swap_chunks(parts, low64)
        for t in range(4):
            rows = dot(chunks[t].astype(bf16), unsort)
            for z in range(EXTENT):
                if z < MARGIN:
                    to, ref = z, low_out
                elif z < MARGIN + DEPTH:
                    to, ref = z - MARGIN, core
                else:
                    to, ref = z - MARGIN - DEPTH, high_out
                to = to * PLANE + t * LANES
                for cls in range(CLASSES):
                    piece = rows[z * 8 + cls * 2 : z * 8 + cls * 2 + 2].astype(bf16)
                    ref[cls, :, to : to + LANES] = piece

    half = HALF // 2
    for step in range(-2, half + 4):
        for stage, lag in (
            (second, 0), (first, 2), (coarse, -1), (lift, -3), (project, -4),
            (mix, -3), (gather, -2), (spread, 0),
        ):
            k = step + lag
            if 0 <= k < half:
                for b in range(len(bricks)):
                    for i in (k, HALF - 1 - k):
                        stage(b * HALF + i)
    emit()


VMEM = pl.BlockSpec(memory_space=pltpu.VMEM)


def evaluate(volume, tissue, w_first, w_second, w_down, w_up, w_out):
    w1 = jnp.transpose(w_first, (1, 2, 3, 4, 0)).reshape(9, 3, CHANNELS)
    w2 = jnp.transpose(w_second, (2, 3, 4, 0, 1)).reshape(27, CHANNELS, CHANNELS)
    wd = jnp.transpose(w_down, (2, 3, 4, 1, 0)).reshape(27, CHANNELS, COARSE)
    edge = jax.ShapeDtypeStruct((CLASSES, OWNED, MARGIN * PLANE), bf16)
    arrays = [pltpu.with_memory_space_constraint(a, pltpu.HBM) for a in (tissue, volume, w1, w2, wd, w_up, w_out)]
    return pl.pallas_call(
        unet,
        out_shape=(jax.ShapeDtypeStruct((CLASSES, OWNED, DEPTH * PLANE), bf16), edge, edge),
        in_specs=[pl.BlockSpec(memory_space=pltpu.HBM)] * 7,
        out_specs=(VMEM,) * 3,
        scratch_shapes=[pltpu.SMEM(tissue.shape, tissue.dtype)]
        + [pltpu.VMEM(a.shape, a.dtype) for a in arrays[1:]]
        + [
            pltpu.SemaphoreType.DMA((7,)),
            pltpu.VMEM((128, 128), f32),
            pltpu.VMEM((4, CHANNELS, 4 * HROWS), f32),
            pltpu.VMEM((3, 256, 128), f32),
            pltpu.VMEM((2 * HROWS, 4 * VROWS), bf16),
            pltpu.VMEM((384, 4 * HROWS), bf16),
            pltpu.VMEM((144, PROWS), bf16),
            pltpu.VMEM((32, 192), bf16),
            pltpu.VMEM((2, 192, 128), f32),
            pltpu.VMEM((OWNED, 2, 26 * VROWS, 128), f32),
            pltpu.VMEM((OWNED, 26 * HROWS, LANES), bf16),
            pltpu.VMEM((OWNED, HALF, 192, LANES), bf16),
            pltpu.VMEM((OWNED * HALF, CHANNELS, LANES), f32),
            pltpu.VMEM((OWNED * HALF, PROWS, LANES), bf16),
            pltpu.VMEM((OWNED, HALF + 2, 144, LANES), f32),
            pltpu.VMEM((OWNED * HALF, COARSE, LANES), bf16),
            pltpu.VMEM((OWNED * HALF, CHANNELS, LANES), f32),
            pltpu.VMEM((OWNED * HALF, 8 * CHANNELS, LANES), bf16),
            pltpu.VMEM((4, 2, EXTENT * 8, 128), f32),
        ],
        compiler_params=pltpu.CompilerParams(vmem_limit_bytes=48 << 20),
    )(*arrays)


def shards(volume, tissue, w_first, w_second, w_down, w_up, w_out):
    core, low, high = evaluate(volume, tissue, w_first, w_second, w_down, w_up, w_out)
    slabs = lax.axis_size("slab")
    me = lax.axis_index("slab")
    odd = (me % 2) == 1
    across = [(i, i + 1) for i in range(1, slabs - 1, 2)] + [(i + 1, i) for i in range(1, slabs - 1, 2)]
    chip = [[i, i + 1] for i in range(0, slabs, 2)]
    two = lax.ppermute(jnp.where(odd, high, low), "slab", across)
    one = lax.all_gather(jnp.where(odd, low, high), "slab", axis_index_groups=chip)
    rest = DEPTH * PLANE - MARGIN * PLANE
    lowest, highest = ((0, 0), (0, 0), (0, rest)), ((0, 0), (0, 0), (rest, 0))

    def place(margin, at):
        return jnp.pad(margin.astype(f32), at)

    total = core.astype(f32)
    total = total + jnp.where(odd, place(one[0], lowest), place(two, lowest))
    total = total + jnp.where(odd, place(two, highest), place(one[1], highest))
    return jnp.transpose(total.astype(bf16), (1, 0, 2))


def solution(mesh):
    return jax.shard_map(
        shards,
        mesh=mesh,
        in_specs=(P(("slab", "work"), None), P(("slab", "work")), P(), P(), P(), P(), P()),
        out_specs=P(("slab", "work"), None, None),
        check_vma=False,
    )
```
